256 devices in a mesh: fac: 8 (over z_lo, core), str: 32 (over x, z_hi, y).
Axes of the slice: x: 4, y: 4, z: 8 (z_hi: 2, z_lo: 4; z = z_hi * 4 + z_lo), core: 2. Of those that a mesh axis runs over, the one named last changes fastest.
Arguments:
- vector: bfloat16 [4096, 8192], P('str'), may hold values from -6 to 6
- alpha_tiles: bfloat16 [8, 4, 128, 128], P('fac'), may hold values from -0.25 to 0.25
- alpha_pattern: int32 [8, 32, 4], P('fac'), may hold values from 0 to 31
- beta_tiles: bfloat16 [8, 4, 128, 128], P('fac'), may hold values from -0.25 to 0.25
- beta_pattern: int32 [8, 64, 4], P('fac'), may hold values from 0 to 63
- alpha_sector: int32 [32], replicated, may hold values from 0 to 1
- beta_sector: int32 [64], replicated, may hold values from 0 to 1
- alpha_diag: float32 [4096], replicated, may hold values from 0.5 to 2
- beta_diag: float32 [8192], replicated, may hold values from 0.5 to 2
- energy: float32 [1], replicated, may hold values from -1 to 0
Outputs:
- first_update: bfloat16 [4096, 8192], P('fac', 'str')
- second_update: bfloat16 [4096, 8192], P('str', 'fac')
The draws below stay inside these ranges and needn't reach their ends.
All inputs are finite; a program needn't handle non-finite values.
Results may differ from the reference program's by a relative error of at most 0.0064.
Values may be sent and summed in bfloat16 or wider, within the bound.
No kernel may reach another device: no remote copies, remote signals or barrier semaphores. Data moves between devices by JAX's collectives and lax.ppermute only.
A program may use at most 64 MiB of HBM per device.

```python
import jax
import jax.numpy as jnp
from jax import lax

NA = 4096
NB = 8192
BLK = 128
S = 4
K = 8
NAB = 32
NBB = 64


def plant(values, key, smallest, high):
    place = [jax.random.randint(jax.random.fold_in(key, axis), (), 0, length) for axis, length in enumerate(values.shape)]
    widest = values.shape.index(max(values.shape))
    beside = place[:widest] + [(place[widest] + 1) % values.shape[widest]] + place[widest + 1:]
    return values.at[tuple(place)].set(smallest).at[tuple(beside)].set(high)


def steps_of(stream_key, dims, split, smallest, high):
    loudness, own = 1.0, jax.random.fold_in(stream_key, 6)
    for dim, parts in split:
        heights = jnp.exp(jax.random.uniform(jax.random.fold_in(own, dim), (parts,), jnp.float32, smallest / len(split), high / len(split)))
        loudness = loudness * jnp.repeat(heights, dims[dim] // parts).reshape([-1 if axis == dim else 1 for axis in range(len(dims))])
    return loudness


def scatter_about(own_key, shape, width, bound, cuts=(), kind=jnp.bfloat16):
    values = width * jax.random.normal(own_key, shape, jnp.float32)
    if cuts:
        values = values * steps_of(own_key, shape, cuts, -0.22, 0.18)
    return jnp.clip(values, -bound, bound).astype(kind)


def setup_inputs(seed: int = 0) -> dict:
    seeds = jax.random.split(jax.random.key(seed), 11)
    return {
        "vector": scatter_about(seeds[0], (NA, NB), 1.0, 6.0, ((0, 32),)),
        "alpha_tiles": scatter_about(seeds[1], (K, S, BLK, BLK), (BLK * S) ** -0.5, 0.25, ((0, 8),)),
        "alpha_pattern": plant(jax.random.randint(seeds[2], (K, NAB, S), 0, NAB), jax.random.fold_in(seeds[2], 1), 0, NAB - 1).astype(jnp.int32),
        "beta_tiles": scatter_about(seeds[3], (K, S, BLK, BLK), (BLK * S) ** -0.5, 0.25, ((0, 8),)),
        "beta_pattern": plant(jax.random.randint(seeds[4], (K, NBB, S), 0, NBB), jax.random.fold_in(seeds[4], 1), 0, NBB - 1).astype(jnp.int32),
        "alpha_sector": plant(jax.random.randint(seeds[5], (NAB,), 0, 2), jax.random.fold_in(seeds[5], 1), 0, 1).astype(jnp.int32),
        "beta_sector": plant(jax.random.randint(seeds[6], (NBB,), 0, 2), jax.random.fold_in(seeds[6], 1), 0, 1).astype(jnp.int32),
        "alpha_diag": jnp.clip(jax.random.uniform(seeds[7], (NA,), jnp.float32, 0.5, 2.0), 0.5, 2.0),
        "beta_diag": jnp.clip(jax.random.uniform(seeds[8], (NB,), jnp.float32, 0.5, 2.0), 0.5, 2.0),
        "energy": jnp.clip(jax.random.uniform(seeds[9], (1,), jnp.float32, -1.0, 0.0), -1.0, 0.0),
    }


def beta_apply(matrix, tile_set, pattern):
    height = matrix.shape[0]
    blocks = matrix.reshape(height, NBB, BLK).astype(jnp.float32)
    picked = jnp.take(blocks, pattern.reshape(-1), axis=1).reshape(height, NBB, S * BLK)
    stacked = tile_set.astype(jnp.float32).reshape(S * BLK, BLK)
    result = jnp.einsum("rjk,kc->rjc", picked, stacked)
    return result.reshape(height, NBB * BLK)


def alpha_apply(matrix, tile_set, pattern):
    breadth = matrix.shape[1]
    blocks = matrix.reshape(NAB, BLK, breadth).astype(jnp.float32)
    picked = jnp.take(blocks, pattern.reshape(-1), axis=0).reshape(NAB, S * BLK, breadth)
    stacked = tile_set.astype(jnp.float32).transpose(1, 0, 2).reshape(BLK, S * BLK)
    result = jnp.einsum("ak,jkc->jac", stacked, picked)
    return result.reshape(NAB * BLK, breadth)


def reference(vector, alpha_tiles, alpha_pattern, beta_tiles, beta_pattern, alpha_sector, beta_sector, alpha_diag, beta_diag, energy):
    live_mask = (jnp.repeat(alpha_sector, BLK)[:, None] == jnp.repeat(beta_sector, BLK)[None, :]).astype(jnp.float32)
    denominator = alpha_diag[:, None] + beta_diag[None, :] - energy[0]

    def forward(running, inputs):
        image = beta_apply(vector, inputs[2], inputs[3]).astype(jnp.bfloat16)
        return running + alpha_apply(image, inputs[0], inputs[1]), None

    factors = (alpha_tiles, alpha_pattern, beta_tiles, beta_pattern)
    sigma_first, _ = lax.scan(forward, jnp.zeros((NA, NB), jnp.float32), factors)
    first_update = (live_mask * sigma_first / denominator).astype(jnp.bfloat16)

    def backward(running, inputs):
        image = alpha_apply(first_update, inputs[0], inputs[1]).astype(jnp.bfloat16)
        return running + beta_apply(image, inputs[2], inputs[3]), None

    sigma_second, _ = lax.scan(backward, jnp.zeros((NA, NB), jnp.float32), factors)
    second_update = (live_mask * sigma_second / denominator).astype(jnp.bfloat16)
    return first_update, second_update
```

```python
import functools
import itertools

import jax
import jax.numpy as jnp
import numpy as np
from jax import lax
from jax.experimental import pallas as pl
from jax.experimental.pallas import tpu as pltpu
from jax.sharding import Mesh
from jax.sharding import PartitionSpec as P

ALL = ("zl", "c", "x", "zh", "y")
FAC = ("zl", "c")
SIZES = (4, 2, 4, 2, 4)
K, S, BLK, NAB, NBB = 8, 4, 128, 32, 64
PAY = 144
f32, bf16 = jnp.float32, jnp.bfloat16

NT = (((1,), (1,)), ((), ()))
NN = (((1,), (0,)), ((), ()))


def permutation(move):
    index = np.arange(256).reshape(SIZES)
    places = itertools.product(*(range(n) for n in SIZES))
    return [(int(index[p]), int(index[move(*p)])) for p in places]


MIRROR = permutation(lambda zl, c, x, zh, y: (3 - zl, c, x, 1 - zh, y))
SIBLING = permutation(lambda zl, c, x, zh, y: (zl, 1 - c, x, zh, y))

VM = pl.BlockSpec(memory_space=pltpu.VMEM)
SM = pl.BlockSpec(memory_space=pltpu.SMEM)


def call(kernel, out_shape, in_specs, scratch=(), mib=40):
    many = isinstance(out_shape, (list, tuple))
    return pl.pallas_call(
        kernel,
        out_shape=out_shape,
        in_specs=in_specs,
        out_specs=[VM] * len(out_shape) if many else VM,
        scratch_shapes=list(scratch),
        compiler_params=pltpu.CompilerParams(vmem_limit_bytes=mib << 20),
    )


def pack_kernel(pos, tiles, bpat, apat, out, turned):
    zh = pos[3]
    for s in range(S):
        turned[s] = tiles[s].astype(f32).T.astype(bf16)
    tail = jnp.concatenate(
        [bpat[...].astype(f32), apat[...].astype(f32), jnp.zeros((13, BLK), f32)], axis=0
    ).astype(bf16)
    for zl in range(4):
        quarter = zl + zh * (3 - 2 * zl)
        for s in range(S):
            part = turned[s, pl.ds(pl.multiple_of(quarter * 32, 32), 32), :]
            for c in range(2):
                out[2 * zl + c, s * 32 : s * 32 + 32, :] = part
        for c in range(2):
            out[2 * zl + c, 128:PAY, :] = tail


def beta_first_kernel(pos, pat, vec, recv, out, prod):
    half = pos[1]
    for g in range(2):
        lhs = recv[4 * g : 4 * g + 4, :128, :].reshape(512, BLK)

        def products(q, carry, lhs=lhs):
            at = pl.multiple_of(q * 256, 256)
            pair = vec[:, pl.ds(at, 256)]
            rhs = jnp.concatenate([pair[:, :BLK], pair[:, BLK:]], axis=0)
            r = lax.dot_general(lhs, rhs, NT, preferred_element_type=f32)
            prod[2 * q] = r[:, :BLK]
            prod[2 * q + 1] = r[:, BLK:]
            return carry

        lax.fori_loop(0, NBB // 2, products, 0)

        def collect(d, carry, g=g):
            x, y = d // 4, d % 4
            for zh in range(2):
                j = 2 * (8 * x + 4 * zh + y) + half
                for k in range(4):
                    base = ((4 * g + k) * NBB + j) * S
                    acc = prod[pat[base], k * 128 : k * 128 + 32, :]
                    for s in range(1, S):
                        acc += prod[pat[base + s], k * 128 + s * 32 : k * 128 + s * 32 + 32, :]
                    out[d, 4 * g + k, zh] = acc.astype(bf16)
            return carry

        lax.fori_loop(0, 16, collect, 0)


def alpha_first_kernel(pos, slot, img, tiles, send, keep, prod, acc):
    zh = pos[3]
    prod[16] = jnp.zeros((64, 512), f32)
    acc[...] = jnp.zeros_like(acc)

    def factor(k, carry):
        rhs = tiles[k].reshape(512, BLK)

        def products(q, carry):
            lhs = img[pl.ds(4 * q, 4), k].reshape(256, BLK)
            r = lax.dot_general(lhs, rhs, NT, preferred_element_type=f32)
            prod[pl.ds(4 * q, 4)] = r.reshape(4, 64, 512)
            return carry

        lax.fori_loop(0, 4, products, 0)

        def collect(i, carry):
            base = (k * NAB + i) * S
            a = acc[i]
            for s in range(S):
                a += prod[slot[base + s], :, s * BLK : s * BLK + BLK]
            acc[i] = a
            return carry

        lax.fori_loop(0, NAB, collect, 0, unroll=2)
        return carry

    lax.fori_loop(0, K, factor, 0)
    own = pl.multiple_of(zh * 32, 32)
    other = pl.multiple_of((1 - zh) * 32, 32)
    keep[...] = acc[:, pl.ds(own, 32), :]
    send[...] = acc[:, pl.ds(other, 32), :].astype(bf16)


def first_kernel(live, keep, recv, adiag, bcol, ua, ub):
    def block(i, carry):
        den = adiag[pl.ds(i, 1), :] + bcol[...]
        u = live[i] * (keep[i] + recv[i].astype(f32)) / den
        u = u.astype(bf16)
        ua[i] = u[:16]
        ub[i] = u[16:]
        return carry

    lax.fori_loop(0, NAB, block, 0)


def alpha_second_kernel(pos, pat, ua, ub, tiles, out, mine, theirs, weight, prod, cols):
    zh, ze, c, zl = pos[3], pos[2], pos[1], pos[0]
    row = pl.multiple_of(ze * 32, 32)
    for k in range(K):
        for s in range(S):
            weight[k * 128 + s * 32 : k * 128 + s * 32 + 32, :] = tiles[k, s, pl.ds(row, 32), :]
    for q in range(4):
        z = q + zh * (3 - 2 * q)
        cols[:, q * 32 : q * 32 + 16, :] = ua[z]
        cols[:, q * 32 + 16 : q * 32 + 32, :] = ub[z]

    def products(q, carry):
        rhs = cols[pl.ds(2 * q, 2)].reshape(256, BLK)
        for g in range(4):
            lhs = weight[g * 256 : g * 256 + 256, :]
            r = lax.dot_general(lhs, rhs, NT, preferred_element_type=f32)
            prod[2 * q, g * 256 : g * 256 + 256, :] = r[:, :BLK]
            prod[2 * q + 1, g * 256 : g * 256 + 256, :] = r[:, BLK:]
        return carry

    lax.fori_loop(0, NAB // 2, products, 0)

    def collect(d, carry):
        x, y = d // 4, d % 4
        for w in range(2):
            i = 8 * x + 4 * w + y
            for k in range(K):
                base = (k * NAB + i) * S
                a = prod[pat[base], k * 128 : k * 128 + 32, :]
                for s in range(1, S):
                    a += prod[pat[base + s], k * 128 + s * 32 : k * 128 + s * 32 + 32, :]
                a = a.astype(bf16)
                out[0, d, k, w] = a[:16]
                out[1, d, k, w] = a[16:]
        return carry

    lax.fori_loop(0, 16, collect, 0)
    for t in range(4):
        own = cols[4 * (2 * zl + c) + t]
        sib = cols[4 * (2 * zl + 1 - c) + t]
        mine[t * BLK : t * BLK + BLK, :] = own.astype(f32).T.astype(bf16)
        theirs[t * BLK : t * BLK + BLK, :] = sib.astype(f32).T.astype(bf16)


def beta_second_kernel(slot, img, tiles, out, prod, acc):
    prod[32] = jnp.zeros((32, 512), f32)
    acc[...] = jnp.zeros_like(acc)

    def factor(k, carry):
        rhs = jnp.concatenate([tiles[k, s] for s in range(S)], axis=1)

        def products(q, carry):
            lhs = img[pl.ds(8 * q, 8), k].reshape(256, BLK)
            r = lax.dot_general(lhs, rhs, NN, preferred_element_type=f32)
            prod[pl.ds(8 * q, 8)] = r.reshape(8, 32, 512)
            return carry

        lax.fori_loop(0, 4, products, 0)

        def collect(j, carry):
            base = (k * NBB + j) * S
            a = acc[j]
            for s in range(S):
                a += prod[slot[base + s], :, s * BLK : s * BLK + BLK]
            acc[j] = a
            return carry

        lax.fori_loop(0, NBB, collect, 0, unroll=4)
        return carry

    lax.fori_loop(0, K, factor, 0)
    for f in range(8):
        part = acc[8 * f : 8 * f + 8].astype(bf16)
        out[f, 0] = part[:, :16]
        out[f, 1] = part[:, 16:]


def second_kernel(live, recv, acol, brow, out):
    for ze in range(4):
        for c in range(2):
            g = 2 * ze + c
            a = acol[16 * g : 16 * g + 16, :]
            for j in range(8):
                one = recv[2 * g, j].astype(f32)
                two = recv[2 * (2 * (3 - ze) + c) + 1, j].astype(f32)
                den = a + brow[:, j * BLK : j * BLK + BLK]
                out[16 * g : 16 * g + 16, j * BLK : j * BLK + BLK] = (
                    live[j] * (one + two) / den
                ).astype(bf16)


def body(
    vector,
    alpha_tiles,
    alpha_pattern,
    beta_tiles,
    beta_pattern,
    alpha_sector,
    beta_sector,
    alpha_diag,
    beta_diag,
    energy,
):
    zl, c, x, zh, y = (lax.axis_index(a) for a in ALL)
    ze = zl + zh * (3 - 2 * zl)
    string = 8 * x + 4 * zh + y
    fac = 2 * zl + c
    pos = jnp.stack([zl, c, ze, zh]).astype(jnp.int32)

    all_alpha = lax.all_gather(alpha_tiles[0], FAC, axis=0, tiled=False)
    all_beta = lax.all_gather(beta_tiles[0], FAC, axis=0, tiled=False)

    packed = call(
        pack_kernel,
        jax.ShapeDtypeStruct((8, PAY, BLK), bf16),
        [SM, VM, VM, VM],
        [pltpu.VMEM((S, BLK, BLK), bf16)],
    )(pos, beta_tiles[0], beta_pattern.reshape(2, BLK), alpha_pattern.reshape(1, BLK))
    recv = lax.all_to_all(packed, FAC, split_axis=0, concat_axis=0, tiled=True)
    pats = recv[:, 128:131, :].astype(jnp.int32)
    bpat = pats[:, :2].reshape(-1)
    apat = pats[:, 2].reshape(-1)
    aslot = jnp.where((apat >> 2) % 2 == zh, ((apat >> 3) << 2) + apat % 4, 16)
    bslot = jnp.where(
        (bpat >> 3) % 2 == zh, (bpat % 2) * 16 + ((bpat >> 4) << 2) + (bpat >> 1) % 4, 32
    )

    image = call(
        beta_first_kernel,
        jax.ShapeDtypeStruct((16, K, 2, 32, BLK), bf16),
        [SM, SM, VM, VM],
        [pltpu.VMEM((NBB, 512, BLK), f32)],
    )(pos, bpat, vector, recv)
    image = lax.all_to_all(image, ("x", "y"), split_axis=0, concat_axis=0, tiled=True)
    send, keep = call(
        alpha_first_kernel,
        [
            jax.ShapeDtypeStruct((NAB, 32, BLK), bf16),
            jax.ShapeDtypeStruct((NAB, 32, BLK), f32),
        ],
        [SM, SM, VM, VM],
        [pltpu.VMEM((17, 64, 512), f32), pltpu.VMEM((NAB, 64, BLK), f32)],
    )(pos, aslot, image, all_alpha)
    got = lax.ppermute(send, ALL, MIRROR)

    block = 2 * string + c
    live = (alpha_sector == lax.dynamic_index_in_dim(beta_sector, block, keepdims=False)).astype(f32)
    bcol = lax.dynamic_slice_in_dim(beta_diag, block * BLK + ze * 32, 32) - energy[0]
    ua, ub = call(
        first_kernel,
        [jax.ShapeDtypeStruct((NAB, 16, BLK), bf16)] * 2,
        [SM, VM, VM, VM, VM],
    )(live, keep, got, alpha_diag.reshape(NAB, BLK), bcol.reshape(32, 1))
    all_ua = lax.all_gather(ua, "zl", axis=0, tiled=False)
    all_ub = lax.all_gather(ub, "zl", axis=0, tiled=False)

    back, mine, theirs = call(
        alpha_second_kernel,
        [
            jax.ShapeDtypeStruct((2, 16, K, 2, 16, BLK), bf16),
            jax.ShapeDtypeStruct((512, BLK), bf16),
            jax.ShapeDtypeStruct((512, BLK), bf16),
        ],
        [SM, SM, VM, VM, VM],
        [
            pltpu.VMEM((K * S * 32, BLK), bf16),
            pltpu.VMEM((NAB, K * S * 32, BLK), f32),
            pltpu.VMEM((NAB, BLK, BLK), bf16),
        ],
    )(pos, apat, all_ua, all_ub, all_alpha)
    other = lax.ppermute(theirs, ALL, SIBLING)
    first_update = jnp.where(
        c == 0,
        jnp.concatenate([mine, other], axis=1),
        jnp.concatenate([other, mine], axis=1),
    )

    back = back.reshape(32, K, 2, 16, BLK)
    back = lax.all_to_all(back, ("c", "x", "y"), split_axis=0, concat_axis=0, tiled=True)
    part = call(
        beta_second_kernel,
        jax.ShapeDtypeStruct((8, 2, 8, 16, BLK), bf16),
        [SM, VM, VM],
        [pltpu.VMEM((33, 32, 512), f32), pltpu.VMEM((NBB, 32, BLK), f32)],
    )(bslot, back, all_beta)
    part = part.reshape(16, 8, 16, BLK)
    part = lax.all_to_all(part, ("zl", "c", "zh"), split_axis=0, concat_axis=0, tiled=True)
    labels = lax.dynamic_slice_in_dim(beta_sector, fac * 8, 8)
    live_cols = (labels == lax.dynamic_index_in_dim(alpha_sector, string, keepdims=False)).astype(f32)
    acol = lax.dynamic_slice_in_dim(alpha_diag, string * BLK, BLK) - energy[0]
    brow = lax.dynamic_slice_in_dim(beta_diag, fac * 1024, 1024)
    second_update = call(
        second_kernel,
        jax.ShapeDtypeStruct((BLK, 1024), bf16),
        [SM, VM, VM, VM],
    )(live_cols, part, acol.reshape(BLK, 1), brow.reshape(1, 1024))
    return (first_update, second_update)


def solution(mesh):
    finer = Mesh(mesh.devices.reshape(SIZES), ALL)
    strings = ("x", "zh", "y")
    in_specs = (
        P(strings, None),
        P(FAC, None, None, None),
        P(FAC, None, None),
        P(FAC, None, None, None),
        P(FAC, None, None),
        P(),
        P(),
        P(),
        P(),
        P(),
    )
    out_specs = (P(FAC, strings), P(strings, FAC))
    return jax.shard_map(body, mesh=finer, in_specs=in_specs, out_specs=out_specs, check_vma=False)
```

```python
import functools
import itertools

import jax
import jax.numpy as jnp
import numpy as np
from jax import lax
from jax.experimental import pallas as pl
from jax.experimental.pallas import tpu as pltpu
from jax.sharding import Mesh
from jax.sharding import PartitionSpec as P

ALL = ("zl", "c", "x", "zh", "y")
FAC = ("zl", "c")
SIZES = (4, 2, 4, 2, 4)
K, S, BLK, NAB, NBB = 8, 4, 128, 32, 64
PAY = 144
f32, bf16 = jnp.float32, jnp.bfloat16

NT = (((1,), (1,)), ((), ()))
NN = (((1,), (0,)), ((), ()))


def permutation(move):
    index = np.arange(256).reshape(SIZES)
    places = itertools.product(*(range(n) for n in SIZES))
    return [(int(index[p]), int(index[move(*p)])) for p in places]


MIRROR = permutation(lambda zl, c, x, zh, y: (3 - zl, c, x, 1 - zh, y))
BESIDE = [permutation(lambda zl, c, x, zh, y, t=t: (zl ^ t, c, x, zh, y)) for t in range(4)]
SIBLING = permutation(lambda zl, c, x, zh, y: (zl, 1 - c, x, zh, y))

VM = pl.BlockSpec(memory_space=pltpu.VMEM)
HB = pl.BlockSpec(memory_space=pl.ANY)
SM = pl.BlockSpec(memory_space=pltpu.SMEM)


def call(kernel, out_shape, in_specs, scratch=(), mib=40, us=2, outs=None):
    many = isinstance(out_shape, (list, tuple))
    return pl.pallas_call(
        kernel,
        out_shape=out_shape,
        in_specs=in_specs,
        out_specs=outs or ([VM] * len(out_shape) if many else VM),
        scratch_shapes=list(scratch),
        cost_estimate=pl.CostEstimate(flops=0, transcendentals=0, bytes_accessed=us * 3_000_000),
        compiler_params=pltpu.CompilerParams(vmem_limit_bytes=mib << 20),
    )


def pack_kernel(pos, alpha, beta, apat, bpat, out, both, raw, turned, tail, sem):
    zh = pos[3]
    copies = [
        pltpu.make_async_copy(beta, raw, sem.at[0]),
        pltpu.make_async_copy(alpha, both.at[pl.ds(0, S)], sem.at[1]),
        pltpu.make_async_copy(beta, both.at[pl.ds(S, S)], sem.at[2]),
    ]
    for copy in copies:
        copy.start()
    one = (
        lax.broadcasted_iota(jnp.int32, (8, S), 0) == lax.broadcasted_iota(jnp.int32, (8, S), 1)
    ).astype(f32)
    tail[...] = jnp.zeros_like(tail)
    tail[:8, :NBB] = lax.dot_general(one, bpat[...].astype(f32), NT, preferred_element_type=f32)
    tail[8:, :NAB] = lax.dot_general(one, apat[...].astype(f32), NT, preferred_element_type=f32)
    last = tail[...].astype(bf16)
    copies[0].wait()
    for s in range(S):
        turned[s] = raw[s].astype(f32).T.astype(bf16)
    for zl in range(4):
        quarter = zl + zh * (3 - 2 * zl)
        for s in range(S):
            part = turned[s, pl.ds(pl.multiple_of(quarter * 32, 32), 32), :]
            for c in range(2):
                out[2 * zl + c, s * 32 : s * 32 + 32, :] = part
        for c in range(2):
            out[2 * zl + c, 128:PAY, :] = last
    for copy in copies[1:]:
        copy.wait()


def beta_first_kernel(chunk, pos, pat, vec, recv, out, prod):
    half = pos[1]
    lhs = jnp.concatenate(
        [
            recv[k, s * 32 + chunk * 16 : s * 32 + chunk * 16 + 16, :]
            for k in range(K)
            for s in range(S)
        ],
        axis=0,
    )

    def products(q, carry):
        pair = vec[:, pl.ds(pl.multiple_of(q * 256, 256), 256)]
        rhs = jnp.concatenate([pair[:, :BLK], pair[:, BLK:]], axis=0)
        r = lax.dot_general(lhs, rhs, NT, preferred_element_type=f32)
        prod[2 * q] = r[:, :BLK]
        prod[2 * q + 1] = r[:, BLK:]
        return carry

    lax.fori_loop(0, NBB // 2, products, 0, unroll=16)

    def collect(d, carry):
        x, y = d // 4, d % 4
        for zh in range(2):
            j = 2 * (8 * x + 4 * zh + y) + half
            for k in range(K):
                base = k * S * NBB + j
                t = [
                    prod[pat[base + s * NBB], k * 64 + s * 16 : k * 64 + s * 16 + 16, :]
                    for s in range(S)
                ]
                out[d, k, zh] = ((t[0] + t[1]) + (t[2] + t[3])).astype(bf16)
        return carry

    lax.fori_loop(0, 16, collect, 0, unroll=2)


def alpha_first_kernel(pos, slot, img, tiles, send, keep, prod, acc):
    zh = pos[3]
    for t in range(2):
        prod[t, 16] = jnp.zeros((32, 512), f32)
    acc[...] = jnp.zeros_like(acc)

    def factors(g, carry):
        for t in range(2):
            rhs = tiles[2 * g + t, :S].reshape(512, BLK)
            for q in range(2):
                lhs = img[8 * q : 8 * q + 8, 2 * g + t].reshape(256, BLK)
                r = lax.dot_general(lhs, rhs, NT, preferred_element_type=f32)
                prod[t, 8 * q : 8 * q + 8] = r.reshape(8, 32, 512)

        def collect(i, carry):
            a = acc[i]
            for t in range(2):
                for s in range(S):
                    at = slot[((2 * g + t) * S + s) * NAB + i]
                    a += prod[t, at, :, s * BLK : s * BLK + BLK]
            acc[i] = a
            return carry

        lax.fori_loop(0, NAB, collect, 0, unroll=8)
        return carry

    lax.fori_loop(0, K // 2, factors, 0)
    own = pl.multiple_of(zh * 16, 16)
    other = pl.multiple_of((1 - zh) * 16, 16)
    keep[...] = acc[:, pl.ds(own, 16), :]
    send[...] = acc[:, pl.ds(other, 16), :].astype(bf16)


def first_kernel(live, keep, recv, adiag, bcol, out):
    def block(i, carry):
        den = adiag[pl.ds(i, 1), :] + bcol[...]
        u = live[i] * (keep[i] + recv[i].astype(f32)) / den
        out[i] = u.astype(bf16)
        return carry

    lax.fori_loop(0, NAB, block, 0, unroll=4)


def alpha_second_kernel(
    pos, pat, u0, u1, u2, u3, v0, v1, v2, v3, tiles, out, mine, theirs, weight, prod, cols
):
    zh, ze, c, zl = pos[3], pos[2], pos[1], pos[0]
    row = pl.multiple_of(ze * 32, 32)
    for k in range(K):
        weight[k] = tiles[k, :S, pl.ds(row, 32), :]
    for t, (ua, ub) in enumerate(((u0, v0), (u1, v1), (u2, v2), (u3, v3))):
        for at in range(4):

            @pl.when(ze == at ^ t)
            def _(ua=ua, ub=ub, at=at):
                cols[:, at * 32 : at * 32 + 16, :] = ua[...]
                cols[:, at * 32 + 16 : at * 32 + 32, :] = ub[...]


    def products(q, carry):
        rhs = cols[pl.ds(2 * q, 2)].reshape(256, BLK)
        for g in range(2):
            lhs = weight[4 * g : 4 * g + 4].reshape(512, BLK)
            r = lax.dot_general(lhs, rhs, NT, preferred_element_type=f32)
            prod[2 * q, g * 512 : g * 512 + 512, :] = r[:, :BLK]
            prod[2 * q + 1, g * 512 : g * 512 + 512, :] = r[:, BLK:]
        return carry

    lax.fori_loop(0, NAB // 2, products, 0, unroll=16)

    def collect(d, carry):
        x, y = d // 4, d % 4
        for w in range(2):
            for k in range(K):
                base = k * S * NAB + 8 * x + 4 * w + y
                a = prod[pat[base], k * 128 : k * 128 + 32, :]
                for s in range(1, S):
                    a += prod[pat[base + s * NAB], k * 128 + s * 32 : k * 128 + s * 32 + 32, :]
                a = a.astype(bf16)
                out[0, d, k, w] = a[:16]
                out[1, d, k, w] = a[16:]
        return carry

    lax.fori_loop(0, 16, collect, 0, unroll=2)
    for t in range(4):
        own = cols[4 * (2 * zl + c) + t]
        sib = cols[4 * (2 * zl + 1 - c) + t]
        mine[t * BLK : t * BLK + BLK, :] = own.astype(f32).T.astype(bf16)
        theirs[t * BLK : t * BLK + BLK, :] = sib.astype(f32).T.astype(bf16)


def beta_second_kernel(slot, img, tiles, out, prod, acc):
    for t in range(2):
        prod[t, 32] = jnp.zeros((32, 512), f32)
    acc[...] = jnp.zeros_like(acc)

    def factors(g, carry):
        for t in range(2):
            rhs = jnp.concatenate([tiles[2 * g + t, S + s] for s in range(S)], axis=1)
            for q in range(4):
                lhs = img[8 * q : 8 * q + 8, 2 * g + t].reshape(256, BLK)
                r = lax.dot_general(lhs, rhs, NN, preferred_element_type=f32)
                prod[t, 8 * q : 8 * q + 8] = r.reshape(8, 32, 512)

        def collect(j, carry):
            a = acc[j]
            for t in range(2):
                for s in range(S):
                    at = slot[((2 * g + t) * S + s) * NBB + j]
                    a += prod[t, at, :, s * BLK : s * BLK + BLK]
            acc[j] = a
            return carry

        lax.fori_loop(0, NBB, collect, 0, unroll=8)
        return carry

    lax.fori_loop(0, K // 2, factors, 0)
    for f in range(8):
        part = acc[8 * f : 8 * f + 8].astype(bf16)
        out[f, 0] = part[:, :16]
        out[f, 1] = part[:, 16:]


def second_kernel(live, recv, acol, brow, out):
    for ze in range(4):
        for c in range(2):
            g = 2 * ze + c
            a = acol[16 * g : 16 * g + 16, :]
            for j in range(8):
                one = recv[2 * g, j].astype(f32)
                two = recv[2 * (2 * (3 - ze) + c) + 1, j].astype(f32)
                den = a + brow[:, j * BLK : j * BLK + BLK]
                out[16 * g : 16 * g + 16, j * BLK : j * BLK + BLK] = (
                    live[j] * (one + two) / den
                ).astype(bf16)


def body(
    vector,
    alpha_tiles,
    alpha_pattern,
    beta_tiles,
    beta_pattern,
    alpha_sector,
    beta_sector,
    alpha_diag,
    beta_diag,
    energy,
):
    zl, c, x, zh, y = (lax.axis_index(a) for a in ALL)
    ze = zl + zh * (3 - 2 * zl)
    string = 8 * x + 4 * zh + y
    fac = 2 * zl + c
    pos = jnp.stack([zl, c, ze, zh]).astype(jnp.int32)

    packed, both = call(
        pack_kernel,
        [
            jax.ShapeDtypeStruct((8, PAY, BLK), bf16),
            jax.ShapeDtypeStruct((2 * S, BLK, BLK), bf16),
        ],
        [SM, HB, HB, VM, VM],
        [
            pltpu.VMEM((S, BLK, BLK), bf16),
            pltpu.VMEM((S, BLK, BLK), bf16),
            pltpu.VMEM((16, BLK), f32),
            pltpu.SemaphoreType.DMA((3,)),
        ],
        us=1,
        mib=8,
        outs=[VM, HB],
    )(pos, alpha_tiles[0], beta_tiles[0], alpha_pattern[0], beta_pattern[0])
    tiles = lax.all_gather(both, FAC, axis=0, tiled=False)
    recv = lax.all_to_all(packed, FAC, split_axis=0, concat_axis=0, tiled=True)
    pats = recv[:, 128:PAY, :].astype(jnp.int32)
    bpat = pats[:, :S, :NBB].reshape(-1)
    apat = pats[:, 8 : 8 + S, :NAB].reshape(-1)
    aslot = jnp.where((apat >> 2) % 2 == zh, ((apat >> 3) << 2) + apat % 4, 16)
    bslot = jnp.where(
        (bpat >> 3) % 2 == zh, (bpat % 2) * 16 + ((bpat >> 4) << 2) + (bpat >> 1) % 4, 32
    )

    block = 2 * string + c
    live = (alpha_sector == lax.dynamic_index_in_dim(beta_sector, block, keepdims=False)).astype(f32)
    bcol = lax.dynamic_slice_in_dim(beta_diag, block * BLK + ze * 32, 32) - energy[0]
    adiag = alpha_diag.reshape(NAB, BLK)

    gathered = []
    for chunk in range(2):
        image = call(
            functools.partial(beta_first_kernel, chunk),
            jax.ShapeDtypeStruct((16, K, 2, 16, BLK), bf16),
            [SM, SM, VM, VM],
            [pltpu.VMEM((NBB, 512, BLK), f32)],
            us=5,
            mib=24,
        )(pos, bpat, vector, recv)
        image = lax.all_to_all(image, ("x", "y"), split_axis=0, concat_axis=0, tiled=True)
        send, keep = call(
            alpha_first_kernel,
            [
                jax.ShapeDtypeStruct((NAB, 16, BLK), bf16),
                jax.ShapeDtypeStruct((NAB, 16, BLK), f32),
            ],
            [SM, SM, VM, VM],
            [pltpu.VMEM((2, 17, 32, 512), f32), pltpu.VMEM((NAB, 32, BLK), f32)],
            us=4,
            mib=12,
        )(pos, aslot, image, tiles)
        got = lax.ppermute(send, ALL, MIRROR)
        u = call(
            first_kernel,
            jax.ShapeDtypeStruct((NAB, 16, BLK), bf16),
            [SM, VM, VM, VM, VM],
            us=1,
            mib=6,
        )(live, keep, got, adiag, bcol[chunk * 16 : chunk * 16 + 16].reshape(16, 1))
        gathered += [u] + [lax.ppermute(u, ALL, BESIDE[t]) for t in (1, 2, 3)]

    back, mine, theirs = call(
        alpha_second_kernel,
        [
            jax.ShapeDtypeStruct((2, 16, K, 2, 16, BLK), bf16),
            jax.ShapeDtypeStruct((512, BLK), bf16),
            jax.ShapeDtypeStruct((512, BLK), bf16),
        ],
        [SM, SM] + [VM] * 9,
        [
            pltpu.VMEM((K, S, 32, BLK), bf16),
            pltpu.VMEM((NAB, K * S * 32, BLK), f32),
            pltpu.VMEM((NAB, BLK, BLK), bf16),
        ],
        us=5,
        mib=28,
    )(pos, apat, *gathered, tiles)
    other = lax.ppermute(theirs, ALL, SIBLING)
    first_update = jnp.where(
        c == 0,
        jnp.concatenate([mine, other], axis=1),
        jnp.concatenate([other, mine], axis=1),
    )

    back = back.reshape(32, K, 2, 16, BLK)
    back = lax.all_to_all(back, ("c", "x", "y"), split_axis=0, concat_axis=0, tiled=True)
    part = call(
        beta_second_kernel,
        jax.ShapeDtypeStruct((8, 2, 8, 16, BLK), bf16),
        [SM, VM, VM],
        [pltpu.VMEM((2, 33, 32, 512), f32), pltpu.VMEM((NBB, 32, BLK), f32)],
        us=7,
        mib=16,
    )(bslot, back, tiles)
    part = part.reshape(16, 8, 16, BLK)
    part = lax.all_to_all(part, ("zl", "c", "zh"), split_axis=0, concat_axis=0, tiled=True)
    labels = lax.dynamic_slice_in_dim(beta_sector, fac * 8, 8)
    live_cols = (labels == lax.dynamic_index_in_dim(alpha_sector, string, keepdims=False)).astype(f32)
    acol = lax.dynamic_slice_in_dim(alpha_diag, string * BLK, BLK) - energy[0]
    brow = lax.dynamic_slice_in_dim(beta_diag, fac * 1024, 1024)
    second_update = call(
        second_kernel,
        jax.ShapeDtypeStruct((BLK, 1024), bf16),
        [SM, VM, VM, VM],
        us=1,
        mib=8,
    )(live_cols, part, acol.reshape(BLK, 1), brow.reshape(1, 1024))
    return (first_update, second_update)


def solution(mesh):
    finer = Mesh(mesh.devices.reshape(SIZES), ALL)
    strings = ("x", "zh", "y")
    in_specs = (
        P(strings, None),
        P(FAC, None, None, None),
        P(FAC, None, None),
        P(FAC, None, None, None),
        P(FAC, None, None),
        P(),
        P(),
        P(),
        P(),
        P(),
    )
    out_specs = (P(FAC, strings), P(strings, FAC))
    return jax.shard_map(body, mesh=finer, in_specs=in_specs, out_specs=out_specs, check_vma=False)
```

```python
import functools
import itertools

import jax
import jax.numpy as jnp
import numpy as np
from jax import lax
from jax.experimental import pallas as pl
from jax.experimental.pallas import tpu as pltpu
from jax.sharding import Mesh
from jax.sharding import PartitionSpec as P

ALL = ("zl", "c", "x", "zh", "y")
FAC = ("zl", "c")
SIZES = (4, 2, 4, 2, 4)
K, S, BLK, NAB, NBB = 8, 4, 128, 32, 64
PAY = 144
f32, bf16 = jnp.float32, jnp.bfloat16

NT = (((1,), (1,)), ((), ()))
NN = (((1,), (0,)), ((), ()))


def permutation(move):
    index = np.arange(256).reshape(SIZES)
    places = itertools.product(*(range(n) for n in SIZES))
    return [(int(index[p]), int(index[move(*p)])) for p in places]


MIRROR = permutation(lambda zl, c, x, zh, y: (3 - zl, c, x, 1 - zh, y))
BESIDE = [permutation(lambda zl, c, x, zh, y, t=t: (zl ^ t, c, x, zh, y)) for t in range(4)]
SIBLING = permutation(lambda zl, c, x, zh, y: (zl, 1 - c, x, zh, y))

VM = pl.BlockSpec(memory_space=pltpu.VMEM)
HB = pl.BlockSpec(memory_space=pl.ANY)
SM = pl.BlockSpec(memory_space=pltpu.SMEM)


def call(kernel, out_shape, in_specs, scratch=(), mib=40, us=2, outs=None):
    many = isinstance(out_shape, (list, tuple))
    return pl.pallas_call(
        kernel,
        out_shape=out_shape,
        in_specs=in_specs,
        out_specs=outs or ([VM] * len(out_shape) if many else VM),
        scratch_shapes=list(scratch),
        cost_estimate=pl.CostEstimate(flops=0, transcendentals=0, bytes_accessed=us * 3_000_000),
        compiler_params=pltpu.CompilerParams(vmem_limit_bytes=mib << 20),
    )


def place(pos, k):
    return 4 * ((k % 2) ^ pos[1]) + ((k // 2) ^ pos[0])


def pack_kernel(pos, alpha, beta, apat, bpat, o0, o1, o2, o3, both, raw, turned, tail, sem):
    ze = pos[2]
    outs = (o0, o1, o2, o3)
    copies = [
        pltpu.make_async_copy(beta, raw, sem.at[0]),
        pltpu.make_async_copy(alpha, both.at[pl.ds(0, S)], sem.at[1]),
        pltpu.make_async_copy(beta, both.at[pl.ds(S, S)], sem.at[2]),
    ]
    for copy in copies:
        copy.start()
    tail[...] = jnp.zeros_like(tail)
    tail[:S, :NBB] = bpat[...].astype(f32)
    tail[8 : 8 + S, :NAB] = apat[...].astype(f32)
    last = tail[...].astype(bf16)
    copies[0].wait()
    for s in range(S):
        turned[s] = raw[s].astype(f32).T.astype(bf16)
    for t in range(4):
        quarter = ze ^ t
        for s in range(S):
            part = turned[s, pl.ds(pl.multiple_of(quarter * 32, 32), 32), :]
            outs[t][s * 32 : s * 32 + 32, :] = part
        outs[t][128:PAY, :] = last
    for copy in copies[1:]:
        copy.wait()


def hold_kernel(vec, out):
    out[...] = vec[...]


def beta_first_kernel(chunk, pos, pat, vec, near, far, out, held, prod):
    half = pos[1]
    for k in range(K):
        t = (k // 2) ^ pos[0]

        @pl.when(half == k % 2)
        def _(k=k, t=t):
            held[k] = near[t]

        @pl.when(half != k % 2)
        def _(k=k, t=t):
            held[k] = far[t]

    lhs = jnp.concatenate(
        [
            held[k, s * 32 + chunk * 16 : s * 32 + chunk * 16 + 16, :]
            for k in range(K)
            for s in range(S)
        ],
        axis=0,
    )

    def products(q, carry):
        pair = vec[:, pl.ds(pl.multiple_of(q * 256, 256), 256)]
        rhs = jnp.concatenate([pair[:, :BLK], pair[:, BLK:]], axis=0)
        r = lax.dot_general(lhs, rhs, NT, preferred_element_type=f32)
        prod[2 * q] = r[:, :BLK]
        prod[2 * q + 1] = r[:, BLK:]
        return carry

    lax.fori_loop(0, NBB // 2, products, 0, unroll=16)
    where = [place(pos, k) for k in range(K)]

    def collect(d, carry):
        x, y = d // 4, d % 4
        for zh in range(2):
            j = 2 * (8 * x + 4 * zh + y) + half
            for k in range(K):
                base = where[k] * S * NBB + j
                t = [
                    prod[pat[base + s * NBB], k * 64 + s * 16 : k * 64 + s * 16 + 16, :]
                    for s in range(S)
                ]
                out[d, k, zh] = ((t[0] + t[1]) + (t[2] + t[3])).astype(bf16)
        return carry

    lax.fori_loop(0, 16, collect, 0, unroll=2)


def alpha_first_kernel(pos, slot, img, tiles, send, keep, prod, acc):
    zh = pos[3]
    for t in range(2):
        prod[t, 16] = jnp.zeros((32, 512), f32)
    acc[...] = jnp.zeros_like(acc)

    def factors(g, carry):
        for t in range(2):
            rhs = tiles[2 * g + t, :S].reshape(512, BLK)
            for q in range(2):
                lhs = img[8 * q : 8 * q + 8, 2 * g + t].reshape(256, BLK)
                r = lax.dot_general(lhs, rhs, NT, preferred_element_type=f32)
                prod[t, 8 * q : 8 * q + 8] = r.reshape(8, 32, 512)

        def collect(i, carry):
            a = acc[i]
            for t in range(2):
                for s in range(S):
                    at = slot[(place(pos, 2 * g + t) * S + s) * NAB + i]
                    a += prod[t, at, :, s * BLK : s * BLK + BLK]
            acc[i] = a
            return carry

        lax.fori_loop(0, NAB, collect, 0, unroll=8)
        return carry

    lax.fori_loop(0, K // 2, factors, 0)
    own = pl.multiple_of(zh * 16, 16)
    other = pl.multiple_of((1 - zh) * 16, 16)
    keep[...] = acc[:, pl.ds(own, 16), :]
    send[...] = acc[:, pl.ds(other, 16), :].astype(bf16)


def first_kernel(chunk, pos, energy, asec, bsec, keep, recv, adiag, bdiag, out):
    string, ze, c = pos[4], pos[2], pos[1]
    block = 2 * string + c
    lane = lax.broadcasted_iota(jnp.int32, (16, BLK), 1)
    want = lax.broadcasted_iota(jnp.int32, (16, BLK), 0) + (ze * 32 + chunk * 16)
    row = bdiag[pl.ds(block, 1), :]
    bcol = jnp.sum(jnp.where(lane == want, row, 0.0), axis=1, keepdims=True) - energy[0]
    label = bsec[block]

    def rows(i, carry):
        den = adiag[pl.ds(i, 1), :] + bcol
        live = jnp.where(asec[i] == label, 1.0, 0.0)
        out[i] = (live * (keep[i] + recv[i].astype(f32)) / den).astype(bf16)
        return carry

    lax.fori_loop(0, NAB, rows, 0, unroll=4)


def alpha_second_kernel(
    pos, pat, u0, u1, u2, u3, v0, v1, v2, v3, tiles, out, mine, theirs, weight, prod, cols
):
    zh, ze, c, zl = pos[3], pos[2], pos[1], pos[0]
    row = pl.multiple_of(ze * 32, 32)
    for k in range(K):
        weight[k] = tiles[k, :S, pl.ds(row, 32), :]
    for t, (ua, ub) in enumerate(((u0, v0), (u1, v1), (u2, v2), (u3, v3))):
        for at in range(4):

            @pl.when(ze == at ^ t)
            def _(ua=ua, ub=ub, at=at):
                cols[:, at * 32 : at * 32 + 16, :] = ua[...]
                cols[:, at * 32 + 16 : at * 32 + 32, :] = ub[...]


    def products(q, carry):
        rhs = cols[pl.ds(2 * q, 2)].reshape(256, BLK)
        for g in range(2):
            lhs = weight[4 * g : 4 * g + 4].reshape(512, BLK)
            r = lax.dot_general(lhs, rhs, NT, preferred_element_type=f32)
            prod[2 * q, g * 512 : g * 512 + 512, :] = r[:, :BLK]
            prod[2 * q + 1, g * 512 : g * 512 + 512, :] = r[:, BLK:]
        return carry

    lax.fori_loop(0, NAB // 2, products, 0, unroll=16)
    where = [place(pos, k) for k in range(K)]

    def collect(d, carry):
        x, y = d // 4, d % 4
        for w in range(2):
            for k in range(K):
                base = where[k] * S * NAB + 8 * x + 4 * w + y
                a = prod[pat[base], k * 128 : k * 128 + 32, :]
                for s in range(1, S):
                    a += prod[pat[base + s * NAB], k * 128 + s * 32 : k * 128 + s * 32 + 32, :]
                a = a.astype(bf16)
                out[0, d, k, w] = a[:16]
                out[1, d, k, w] = a[16:]
        return carry

    lax.fori_loop(0, 16, collect, 0, unroll=2)
    for t in range(4):
        own = cols[4 * (2 * zl + c) + t]
        sib = cols[4 * (2 * zl + 1 - c) + t]
        mine[t * BLK : t * BLK + BLK, :] = own.astype(f32).T.astype(bf16)
        theirs[t * BLK : t * BLK + BLK, :] = sib.astype(f32).T.astype(bf16)


def beta_second_kernel(pos, slot, img, tiles, out, prod, acc):
    for t in range(2):
        prod[t, 32] = jnp.zeros((32, 512), f32)
    acc[...] = jnp.zeros_like(acc)

    def factors(g, carry):
        for t in range(2):
            rhs = jnp.concatenate([tiles[2 * g + t, S + s] for s in range(S)], axis=1)
            for q in range(4):
                lhs = img[8 * q : 8 * q + 8, 2 * g + t].reshape(256, BLK)
                r = lax.dot_general(lhs, rhs, NN, preferred_element_type=f32)
                prod[t, 8 * q : 8 * q + 8] = r.reshape(8, 32, 512)

        def collect(j, carry):
            a = acc[j]
            for t in range(2):
                for s in range(S):
                    at = slot[(place(pos, 2 * g + t) * S + s) * NBB + j]
                    a += prod[t, at, :, s * BLK : s * BLK + BLK]
            acc[j] = a
            return carry

        lax.fori_loop(0, NBB, collect, 0, unroll=8)
        return carry

    lax.fori_loop(0, K // 2, factors, 0)
    for f in range(8):
        part = acc[8 * f : 8 * f + 8].astype(bf16)
        out[f, 0] = part[:, :16]
        out[f, 1] = part[:, 16:]


def second_kernel(live, recv, acol, brow, out):
    for ze in range(4):
        for c in range(2):
            g = 2 * ze + c
            a = acol[16 * g : 16 * g + 16, :]
            for j in range(8):
                one = recv[2 * g, j].astype(f32)
                two = recv[2 * (2 * (3 - ze) + c) + 1, j].astype(f32)
                den = a + brow[:, j * BLK : j * BLK + BLK]
                out[16 * g : 16 * g + 16, j * BLK : j * BLK + BLK] = (
                    live[j] * (one + two) / den
                ).astype(bf16)


def body(
    vector,
    alpha_tiles,
    alpha_pattern,
    beta_tiles,
    beta_pattern,
    alpha_sector,
    beta_sector,
    alpha_diag,
    beta_diag,
    energy,
):
    zl, c, x, zh, y = (lax.axis_index(a) for a in ALL)
    ze = zl + zh * (3 - 2 * zl)
    string = 8 * x + 4 * zh + y
    fac = 2 * zl + c
    pos = jnp.stack([zl, c, ze, zh, string]).astype(jnp.int32)

    *packed, both = call(
        pack_kernel,
        [jax.ShapeDtypeStruct((PAY, BLK), bf16)] * 4
        + [jax.ShapeDtypeStruct((2 * S, BLK, BLK), bf16)],
        [SM, HB, HB, VM, VM],
        [
            pltpu.VMEM((S, BLK, BLK), bf16),
            pltpu.VMEM((S, BLK, BLK), bf16),
            pltpu.VMEM((16, BLK), f32),
            pltpu.SemaphoreType.DMA((3,)),
        ],
        us=1,
        mib=8,
        outs=[VM] * 4 + [HB],
    )(pos, alpha_tiles[0], beta_tiles[0], alpha_pattern[0].T, beta_pattern[0].T)
    tiles = lax.all_gather(both, FAC, axis=0, tiled=False)
    near = [packed[0]] + [lax.ppermute(packed[t], ALL, BESIDE[t]) for t in (1, 2, 3)]
    near = jnp.stack(near)
    far = lax.ppermute(near, ALL, SIBLING)
    vector = call(hold_kernel, jax.ShapeDtypeStruct((BLK, NBB * BLK), bf16), [VM], us=2, mib=6)(vector)
    pats = jnp.concatenate([near[:, 128:PAY], far[:, 128:PAY]], axis=0).astype(jnp.int32)
    bpat = pats[:, :S, :NBB].reshape(-1)
    apat = pats[:, 8 : 8 + S, :NAB].reshape(-1)
    aslot = jnp.where((apat >> 2) % 2 == zh, ((apat >> 3) << 2) + apat % 4, 16)
    bslot = jnp.where(
        (bpat >> 3) % 2 == zh, (bpat % 2) * 16 + ((bpat >> 4) << 2) + (bpat >> 1) % 4, 32
    )

    adiag = alpha_diag.reshape(NAB, BLK)
    bdiag = beta_diag.reshape(NBB, BLK)

    gathered = []
    for chunk in range(2):
        image = call(
            functools.partial(beta_first_kernel, chunk),
            jax.ShapeDtypeStruct((16, K, 2, 16, BLK), bf16),
            [SM, SM, VM, VM, VM],
            [pltpu.VMEM((K, PAY, BLK), bf16), pltpu.VMEM((NBB, 512, BLK), f32)],
            us=5,
            mib=24,
        )(pos, bpat, vector, near, far)
        image = lax.all_to_all(image, ("x", "y"), split_axis=0, concat_axis=0, tiled=True)
        send, keep = call(
            alpha_first_kernel,
            [
                jax.ShapeDtypeStruct((NAB, 16, BLK), bf16),
                jax.ShapeDtypeStruct((NAB, 16, BLK), f32),
            ],
            [SM, SM, VM, VM],
            [pltpu.VMEM((2, 17, 32, 512), f32), pltpu.VMEM((NAB, 32, BLK), f32)],
            us=4,
            mib=12,
        )(pos, aslot, image, tiles)
        got = lax.ppermute(send, ALL, MIRROR)
        u = call(
            functools.partial(first_kernel, chunk),
            jax.ShapeDtypeStruct((NAB, 16, BLK), bf16),
            [SM, SM, SM, SM, VM, VM, VM, VM],
            us=1,
            mib=6,
        )(pos, energy, alpha_sector, beta_sector, keep, got, adiag, bdiag)
        one, two = (lax.ppermute(u, ALL, BESIDE[t]) for t in (1, 2))
        gathered += [u, one, two, lax.ppermute(two, ALL, BESIDE[1])]

    back, mine, theirs = call(
        alpha_second_kernel,
        [
            jax.ShapeDtypeStruct((2, 16, K, 2, 16, BLK), bf16),
            jax.ShapeDtypeStruct((512, BLK), bf16),
            jax.ShapeDtypeStruct((512, BLK), bf16),
        ],
        [SM, SM] + [VM] * 9,
        [
            pltpu.VMEM((K, S, 32, BLK), bf16),
            pltpu.VMEM((NAB, K * S * 32, BLK), f32),
            pltpu.VMEM((NAB, BLK, BLK), bf16),
        ],
        us=5,
        mib=28,
    )(pos, apat, *gathered, tiles)
    other = lax.ppermute(theirs, ALL, SIBLING)
    first_update = jnp.where(
        c == 0,
        jnp.concatenate([mine, other], axis=1),
        jnp.concatenate([other, mine], axis=1),
    )

    back = back.reshape(32, K, 2, 16, BLK)
    back = lax.all_to_all(back, ("c", "x", "y"), split_axis=0, concat_axis=0, tiled=True)
    part = call(
        beta_second_kernel,
        jax.ShapeDtypeStruct((8, 2, 8, 16, BLK), bf16),
        [SM, SM, VM, VM],
        [pltpu.VMEM((2, 33, 32, 512), f32), pltpu.VMEM((NBB, 32, BLK), f32)],
        us=7,
        mib=16,
    )(pos, bslot, back, tiles)
    part = part.reshape(16, 8, 16, BLK)
    part = lax.all_to_all(part, ("zl", "c", "zh"), split_axis=0, concat_axis=0, tiled=True)
    labels = lax.dynamic_slice_in_dim(beta_sector, fac * 8, 8)
    live_cols = (labels == lax.dynamic_index_in_dim(alpha_sector, string, keepdims=False)).astype(f32)
    acol = lax.dynamic_slice_in_dim(alpha_diag, string * BLK, BLK) - energy[0]
    brow = lax.dynamic_slice_in_dim(beta_diag, fac * 1024, 1024)
    second_update = call(
        second_kernel,
        jax.ShapeDtypeStruct((BLK, 1024), bf16),
        [SM, VM, VM, VM],
        us=1,
        mib=8,
    )(live_cols, part, acol.reshape(BLK, 1), brow.reshape(1, 1024))
    return (first_update, second_update)


def solution(mesh):
    finer = Mesh(mesh.devices.reshape(SIZES), ALL)
    strings = ("x", "zh", "y")
    in_specs = (
        P(strings, None),
        P(FAC, None, None, None),
        P(FAC, None, None),
        P(FAC, None, None, None),
        P(FAC, None, None),
        P(),
        P(),
        P(),
        P(),
        P(),
    )
    out_specs = (P(FAC, strings), P(strings, FAC))
    return jax.shard_map(body, mesh=finer, in_specs=in_specs, out_specs=out_specs, check_vma=False)
```

```python
import functools
import itertools

import jax
import jax.numpy as jnp
import numpy as np
from jax import lax
from jax.experimental import pallas as pl
from jax.experimental.pallas import tpu as pltpu
from jax.sharding import Mesh
from jax.sharding import PartitionSpec as P

ALL = ("zl", "c", "x", "zh", "y")
FAC = ("zl", "c")
SIZES = (4, 2, 4, 2, 4)
K, S, BLK, NAB, NBB = 8, 4, 128, 32, 64
PAY = 144
f32, bf16 = jnp.float32, jnp.bfloat16

NT = (((1,), (1,)), ((), ()))
NN = (((1,), (0,)), ((), ()))


def permutation(move):
    index = np.arange(256).reshape(SIZES)
    places = itertools.product(*(range(n) for n in SIZES))
    return [(int(index[p]), int(index[move(*p)])) for p in places]


MIRROR = permutation(lambda zl, c, x, zh, y: (3 - zl, c, x, 1 - zh, y))
BESIDE = [permutation(lambda zl, c, x, zh, y, t=t: (zl ^ t, c, x, zh, y)) for t in range(4)]
SIBLING = permutation(lambda zl, c, x, zh, y: (zl, 1 - c, x, zh, y))

VM = pl.BlockSpec(memory_space=pltpu.VMEM)
HB = pl.BlockSpec(memory_space=pl.ANY)
SM = pl.BlockSpec(memory_space=pltpu.SMEM)


def call(kernel, out_shape, in_specs, scratch=(), mib=40, us=2, outs=None):
    many = isinstance(out_shape, (list, tuple))
    return pl.pallas_call(
        kernel,
        out_shape=out_shape,
        in_specs=in_specs,
        out_specs=outs or ([VM] * len(out_shape) if many else VM),
        scratch_shapes=list(scratch),
        cost_estimate=pl.CostEstimate(flops=0, transcendentals=0, bytes_accessed=us * 3_000_000),
        compiler_params=pltpu.CompilerParams(vmem_limit_bytes=mib << 20),
    )


def place(pos, k):
    return 4 * ((k % 2) ^ pos[1]) + ((k // 2) ^ pos[0])


def pack_kernel(pos, alpha, beta, apat, bpat, o0, o1, o2, o3, both, turned, tail, sem):
    ze = pos[2]
    outs = (o0, o1, o2, o3)
    copies = [
        pltpu.make_async_copy(alpha, both.at[pl.ds(0, S)], sem.at[0]),
        pltpu.make_async_copy(beta, both.at[pl.ds(S, S)], sem.at[1]),
    ]
    for copy in copies:
        copy.start()
    tail[...] = jnp.zeros_like(tail)
    tail[:S, :NBB] = bpat[...].astype(f32)
    tail[8 : 8 + S, :NAB] = apat[...].astype(f32)
    last = tail[...].astype(bf16)
    for copy in copies:
        copy.wait()
    for s in range(S):
        turned[s] = both[S + s].astype(f32).T.astype(bf16)
    for t in range(4):
        quarter = ze ^ t
        for s in range(S):
            part = turned[s, pl.ds(pl.multiple_of(quarter * 32, 32), 32), :]
            outs[t][s * 32 : s * 32 + 32, :] = part
        outs[t][128:PAY, :] = last


def hold_kernel(vec, out):
    out[...] = vec[...]


def beta_first_kernel(chunk, pos, pat, vec, near, far, out, held, prod):
    half = pos[1]
    for k in range(K):
        t = (k // 2) ^ pos[0]

        @pl.when(half == k % 2)
        def _(k=k, t=t):
            held[k] = near[t]

        @pl.when(half != k % 2)
        def _(k=k, t=t):
            held[k] = far[t]

    lhs = jnp.concatenate(
        [
            held[k, s * 32 + chunk * 16 : s * 32 + chunk * 16 + 16, :]
            for k in range(K)
            for s in range(S)
        ],
        axis=0,
    )

    def products(q, carry):
        pair = vec[:, pl.ds(pl.multiple_of(q * 256, 256), 256)]
        rhs = jnp.concatenate([pair[:, :BLK], pair[:, BLK:]], axis=0)
        r = lax.dot_general(lhs, rhs, NT, preferred_element_type=f32)
        prod[2 * q] = r[:, :BLK]
        prod[2 * q + 1] = r[:, BLK:]
        return carry

    lax.fori_loop(0, NBB // 2, products, 0, unroll=16)
    where = [place(pos, k) * (S * NBB) for k in range(K)]

    def collect(d, carry):
        x, y = d // 4, d % 4
        for zh in range(2):
            j = 2 * (8 * x + 4 * zh + y) + half
            for k in range(K):
                base = where[k] + j
                t = [
                    prod[pat[base + s * NBB], k * 64 + s * 16 : k * 64 + s * 16 + 16, :]
                    for s in range(S)
                ]
                out[d, k, zh] = ((t[0] + t[1]) + (t[2] + t[3])).astype(bf16)
        return carry

    lax.fori_loop(0, 16, collect, 0, unroll=2)


def alpha_first_kernel(pos, slot, img, tiles, send, keep, prod, acc):
    zh = pos[3]
    for t in range(2):
        prod[t, 16] = jnp.zeros((32, 512), f32)
    acc[...] = jnp.zeros_like(acc)

    def factors(g, carry):
        for t in range(2):
            rhs = tiles[2 * g + t, :S].reshape(512, BLK)
            for q in range(2):
                lhs = img[8 * q : 8 * q + 8, 2 * g + t].reshape(256, BLK)
                r = lax.dot_general(lhs, rhs, NT, preferred_element_type=f32)
                prod[t, 8 * q : 8 * q + 8] = r.reshape(8, 32, 512)

        bases = [place(pos, 2 * g + t) * (S * NAB) for t in range(2)]

        def collect(i, carry):
            a = acc[i]
            for t in range(2):
                for s in range(S):
                    at = slot[bases[t] + s * NAB + i]
                    a += prod[t, at, :, s * BLK : s * BLK + BLK]
            acc[i] = a
            return carry

        lax.fori_loop(0, NAB, collect, 0, unroll=8)
        return carry

    lax.fori_loop(0, K // 2, factors, 0)
    own = pl.multiple_of(zh * 16, 16)
    other = pl.multiple_of((1 - zh) * 16, 16)
    keep[...] = acc[:, pl.ds(own, 16), :]
    send[...] = acc[:, pl.ds(other, 16), :].astype(bf16)


def first_kernel(chunk, pos, energy, asec, bsec, keep, recv, adiag, bdiag, out):
    string, ze, c = pos[4], pos[2], pos[1]
    block = 2 * string + c
    lane = lax.broadcasted_iota(jnp.int32, (16, BLK), 1)
    want = lax.broadcasted_iota(jnp.int32, (16, BLK), 0) + (ze * 32 + chunk * 16)
    row = bdiag[pl.ds(block, 1), :]
    bcol = jnp.sum(jnp.where(lane == want, row, 0.0), axis=1, keepdims=True) - energy[0]
    label = bsec[block]

    def rows(i, carry):
        den = adiag[pl.ds(i, 1), :] + bcol
        live = jnp.where(asec[i] == label, 1.0, 0.0)
        out[i] = (live * (keep[i] + recv[i].astype(f32)) / den).astype(bf16)
        return carry

    lax.fori_loop(0, NAB, rows, 0, unroll=4)


def alpha_second_kernel(
    pos, pat, u0, u1, u2, u3, v0, v1, v2, v3, tiles, out, weight, prod, cols
):
    zh, ze, zl = pos[3], pos[2], pos[0]
    row = pl.multiple_of(ze * 32, 32)
    for k in range(K):
        weight[k] = tiles[k, :S, pl.ds(row, 32), :]
    for t, (ua, ub) in enumerate(((u0, v0), (u1, v1), (u2, v2), (u3, v3))):
        for at in range(4):

            @pl.when(ze == at ^ t)
            def _(ua=ua, ub=ub, at=at):
                cols[:, at * 32 : at * 32 + 16, :] = ua[...]
                cols[:, at * 32 + 16 : at * 32 + 32, :] = ub[...]


    def products(q, carry):
        rhs = cols[pl.ds(2 * q, 2)].reshape(256, BLK)
        for g in range(2):
            lhs = weight[4 * g : 4 * g + 4].reshape(512, BLK)
            r = lax.dot_general(lhs, rhs, NT, preferred_element_type=f32)
            prod[2 * q, g * 512 : g * 512 + 512, :] = r[:, :BLK]
            prod[2 * q + 1, g * 512 : g * 512 + 512, :] = r[:, BLK:]
        return carry

    lax.fori_loop(0, NAB // 2, products, 0, unroll=16)
    where = [place(pos, k) * (S * NAB) for k in range(K)]

    def collect(d, carry):
        x, y = d // 4, d % 4
        for w in range(2):
            for k in range(K):
                base = where[k] + (8 * x + 4 * w + y)
                a = prod[pat[base], k * 128 : k * 128 + 32, :]
                for s in range(1, S):
                    a += prod[pat[base + s * NAB], k * 128 + s * 32 : k * 128 + s * 32 + 32, :]
                a = a.astype(bf16)
                out[d, k, w] = a[:16]
                out[16 + d, k, w] = a[16:]
        return carry

    lax.fori_loop(0, 16, collect, 0, unroll=2)

def edge_kernel(pos, u0, u1, u2, u3, v0, v1, v2, v3, mine, theirs, cols):
    zl, c, ze = pos[0], pos[1], pos[2]
    for out, core in ((mine, c), (theirs, 1 - c)):
        first = 4 * (2 * zl + core)
        for t, (ua, ub) in enumerate(((u0, v0), (u1, v1), (u2, v2), (u3, v3))):
            for at in range(4):

                @pl.when(ze == at ^ t)
                def _(ua=ua, ub=ub, at=at, first=first):
                    cols[:, at * 32 : at * 32 + 16, :] = ua[pl.ds(first, 4)]
                    cols[:, at * 32 + 16 : at * 32 + 32, :] = ub[pl.ds(first, 4)]

        for t in range(4):
            out[t * BLK : t * BLK + BLK, :] = cols[t].astype(f32).T.astype(bf16)


def beta_second_kernel(pos, slot, img, tiles, out, prod, acc):
    for t in range(2):
        prod[t, 32] = jnp.zeros((32, 512), f32)
    acc[...] = jnp.zeros_like(acc)

    def factors(g, carry):
        for t in range(2):
            rhs = jnp.concatenate([tiles[2 * g + t, S + s] for s in range(S)], axis=1)
            for q in range(4):
                lhs = img[8 * q : 8 * q + 8, 2 * g + t].reshape(256, BLK)
                r = lax.dot_general(lhs, rhs, NN, preferred_element_type=f32)
                prod[t, 8 * q : 8 * q + 8] = r.reshape(8, 32, 512)

        bases = [place(pos, 2 * g + t) * (S * NBB) for t in range(2)]

        def collect(j, carry):
            a = acc[j]
            for t in range(2):
                for s in range(S):
                    at = slot[bases[t] + s * NBB + j]
                    a += prod[t, at, :, s * BLK : s * BLK + BLK]
            acc[j] = a
            return carry

        lax.fori_loop(0, NBB, collect, 0, unroll=8)
        return carry

    lax.fori_loop(0, K // 2, factors, 0)
    for f in range(8):
        part = acc[8 * f : 8 * f + 8].astype(bf16)
        out[f, 0] = part[:, :16]
        out[f, 1] = part[:, 16:]


def second_kernel(live, recv, acol, brow, out):
    for ze in range(4):
        for c in range(2):
            g = 2 * ze + c
            a = acol[16 * g : 16 * g + 16, :]
            for j in range(8):
                one = recv[2 * g, j].astype(f32)
                two = recv[2 * (2 * (3 - ze) + c) + 1, j].astype(f32)
                den = a + brow[:, j * BLK : j * BLK + BLK]
                out[16 * g : 16 * g + 16, j * BLK : j * BLK + BLK] = (
                    live[j] * (one + two) / den
                ).astype(bf16)


def body(
    vector,
    alpha_tiles,
    alpha_pattern,
    beta_tiles,
    beta_pattern,
    alpha_sector,
    beta_sector,
    alpha_diag,
    beta_diag,
    energy,
):
    zl, c, x, zh, y = (lax.axis_index(a) for a in ALL)
    ze = zl + zh * (3 - 2 * zl)
    string = 8 * x + 4 * zh + y
    fac = 2 * zl + c
    pos = jnp.stack([zl, c, ze, zh, string]).astype(jnp.int32)

    *packed, both = call(
        pack_kernel,
        [jax.ShapeDtypeStruct((PAY, BLK), bf16)] * 4
        + [jax.ShapeDtypeStruct((2 * S, BLK, BLK), bf16)],
        [SM, HB, HB, VM, VM],
        [
            pltpu.VMEM((S, BLK, BLK), bf16),
            pltpu.VMEM((16, BLK), f32),
            pltpu.SemaphoreType.DMA((2,)),
        ],
        us=1,
        mib=58,
    )(pos, alpha_tiles[0], beta_tiles[0], alpha_pattern[0].T, beta_pattern[0].T)
    tiles = lax.all_gather(both, FAC, axis=0, tiled=False)
    near = [packed[0]] + [lax.ppermute(packed[t], ALL, BESIDE[t]) for t in (1, 2, 3)]
    near = jnp.stack(near)
    vector = call(hold_kernel, jax.ShapeDtypeStruct((BLK, NBB * BLK), bf16), [VM], us=2, mib=6)(vector)
    near, vector = lax.optimization_barrier((near, vector))
    far = lax.ppermute(near, ALL, SIBLING)
    pats = jnp.concatenate([near[:, 128:PAY], far[:, 128:PAY]], axis=0).astype(jnp.int32)
    bpat = pats[:, :S, :NBB].reshape(-1)
    apat = pats[:, 8 : 8 + S, :NAB].reshape(-1)
    aslot = jnp.where((apat >> 2) % 2 == zh, ((apat >> 3) << 2) + apat % 4, 16)
    bslot = jnp.where(
        (bpat >> 3) % 2 == zh, (bpat % 2) * 16 + ((bpat >> 4) << 2) + (bpat >> 1) % 4, 32
    )

    adiag = alpha_diag.reshape(NAB, BLK)
    bdiag = beta_diag.reshape(NBB, BLK)

    gathered = []
    for chunk in range(2):
        image = call(
            functools.partial(beta_first_kernel, chunk),
            jax.ShapeDtypeStruct((16, K, 2, 16, BLK), bf16),
            [SM, SM, VM, VM, VM],
            [pltpu.VMEM((K, PAY, BLK), bf16), pltpu.VMEM((NBB, 512, BLK), f32)],
            us=5,
            mib=24,
        )(pos, bpat, vector, near, far)
        image = lax.all_to_all(image, ("x", "y"), split_axis=0, concat_axis=0, tiled=True)
        send, keep = call(
            alpha_first_kernel,
            [
                jax.ShapeDtypeStruct((NAB, 16, BLK), bf16),
                jax.ShapeDtypeStruct((NAB, 16, BLK), f32),
            ],
            [SM, SM, VM, VM],
            [pltpu.VMEM((2, 17, 32, 512), f32), pltpu.VMEM((NAB, 32, BLK), f32)],
            us=4,
            mib=12,
        )(pos, aslot, image, tiles)
        got = lax.ppermute(send, ALL, MIRROR)
        u = call(
            functools.partial(first_kernel, chunk),
            jax.ShapeDtypeStruct((NAB, 16, BLK), bf16),
            [SM, SM, SM, SM, VM, VM, VM, VM],
            us=1,
            mib=6,
        )(pos, energy, alpha_sector, beta_sector, keep, got, adiag, bdiag)
        one, two = (lax.ppermute(u, ALL, BESIDE[t]) for t in (1, 2))
        gathered += [u, one, two, lax.ppermute(two, ALL, BESIDE[1])]

    mine, theirs = call(
        edge_kernel,
        [jax.ShapeDtypeStruct((512, BLK), bf16)] * 2,
        [SM] + [VM] * 8,
        [pltpu.VMEM((4, BLK, BLK), bf16)],
        us=1,
        mib=6,
    )(pos, *gathered)
    back = call(
        alpha_second_kernel,
        jax.ShapeDtypeStruct((32, K, 2, 16, BLK), bf16),
        [SM, SM] + [VM] * 9,
        [
            pltpu.VMEM((K, S, 32, BLK), bf16),
            pltpu.VMEM((NAB, K * S * 32, BLK), f32),
            pltpu.VMEM((NAB, BLK, BLK), bf16),
        ],
        us=5,
        mib=28,
    )(pos, apat, *gathered, tiles)
    other = lax.ppermute(theirs, ALL, SIBLING)
    first_update = jnp.where(
        c == 0,
        jnp.concatenate([mine, other], axis=1),
        jnp.concatenate([other, mine], axis=1),
    )

    back = lax.all_to_all(back, ("c", "x", "y"), split_axis=0, concat_axis=0, tiled=True)
    part = call(
        beta_second_kernel,
        jax.ShapeDtypeStruct((8, 2, 8, 16, BLK), bf16),
        [SM, SM, VM, VM],
        [pltpu.VMEM((2, 33, 32, 512), f32), pltpu.VMEM((NBB, 32, BLK), f32)],
        us=7,
        mib=16,
    )(pos, bslot, back, tiles)
    part = part.reshape(16, 8, 16, BLK)
    part = lax.all_to_all(part, ("zl", "c", "zh"), split_axis=0, concat_axis=0, tiled=True)
    labels = lax.dynamic_slice_in_dim(beta_sector, fac * 8, 8)
    live_cols = (labels == lax.dynamic_index_in_dim(alpha_sector, string, keepdims=False)).astype(f32)
    acol = lax.dynamic_slice_in_dim(alpha_diag, string * BLK, BLK) - energy[0]
    brow = lax.dynamic_slice_in_dim(beta_diag, fac * 1024, 1024)
    second_update = call(
        second_kernel,
        jax.ShapeDtypeStruct((BLK, 1024), bf16),
        [SM, VM, VM, VM],
        us=1,
        mib=8,
    )(live_cols, part, acol.reshape(BLK, 1), brow.reshape(1, 1024))
    return (first_update, second_update)


def solution(mesh):
    finer = Mesh(mesh.devices.reshape(SIZES), ALL)
    strings = ("x", "zh", "y")
    in_specs = (
        P(strings, None),
        P(FAC, None, None, None),
        P(FAC, None, None),
        P(FAC, None, None, None),
        P(FAC, None, None),
        P(),
        P(),
        P(),
        P(),
        P(),
    )
    out_specs = (P(FAC, strings), P(strings, FAC))
    return jax.shard_map(body, mesh=finer, in_specs=in_specs, out_specs=out_specs, check_vma=False)
```

```python
import functools
import itertools

import jax
import jax.numpy as jnp
import numpy as np
from jax import lax
from jax.experimental import pallas as pl
from jax.experimental.pallas import tpu as pltpu
from jax.sharding import Mesh
from jax.sharding import PartitionSpec as P

ALL = ("zl", "c", "x", "zh", "y")
FAC = ("zl", "c")
SIZES = (4, 2, 4, 2, 4)
K, S, BLK, NAB, NBB = 8, 4, 128, 32, 64
PAY = 144
f32, bf16 = jnp.float32, jnp.bfloat16

NT = (((1,), (1,)), ((), ()))
NN = (((1,), (0,)), ((), ()))


def permutation(move):
    index = np.arange(256).reshape(SIZES)
    places = itertools.product(*(range(n) for n in SIZES))
    return [(int(index[p]), int(index[move(*p)])) for p in places]


MIRROR = permutation(lambda zl, c, x, zh, y: (3 - zl, c, x, 1 - zh, y))
BESIDE = [permutation(lambda zl, c, x, zh, y, t=t: (zl ^ t, c, x, zh, y)) for t in range(4)]
SIBLING = permutation(lambda zl, c, x, zh, y: (zl, 1 - c, x, zh, y))

VM = pl.BlockSpec(memory_space=pltpu.VMEM)
HB = pl.BlockSpec(memory_space=pl.ANY)
SM = pl.BlockSpec(memory_space=pltpu.SMEM)


def call(kernel, out_shape, in_specs, scratch=(), mib=40, us=2, outs=None):
    many = isinstance(out_shape, (list, tuple))
    return pl.pallas_call(
        kernel,
        out_shape=out_shape,
        in_specs=in_specs,
        out_specs=outs or ([VM] * len(out_shape) if many else VM),
        scratch_shapes=list(scratch),
        cost_estimate=pl.CostEstimate(flops=0, transcendentals=0, bytes_accessed=us * 3_000_000),
        compiler_params=pltpu.CompilerParams(vmem_limit_bytes=mib << 20),
    )


def place(pos, k):
    return 4 * ((k % 2) ^ pos[1]) + ((k // 2) ^ pos[0])


def pack_kernel(pos, alpha, beta, apat, bpat, o0, o1, o2, o3, both, turned, tail, sem):
    ze = pos[2]
    outs = (o0, o1, o2, o3)
    copies = [
        pltpu.make_async_copy(alpha, both.at[pl.ds(0, S)], sem.at[0]),
        pltpu.make_async_copy(beta, both.at[pl.ds(S, S)], sem.at[1]),
    ]
    for copy in copies:
        copy.start()
    tail[...] = jnp.zeros_like(tail)
    tail[:S, :NBB] = bpat[...].astype(f32)
    tail[8 : 8 + S, :NAB] = apat[...].astype(f32)
    last = tail[...].astype(bf16)
    for copy in copies:
        copy.wait()
    for s in range(S):
        turned[s] = both[S + s].astype(f32).T.astype(bf16)
    for t in range(4):
        quarter = ze ^ t
        for s in range(S):
            part = turned[s, pl.ds(pl.multiple_of(quarter * 32, 32), 32), :]
            outs[t][s * 32 : s * 32 + 32, :] = part
        outs[t][128:PAY, :] = last


def hold_kernel(vec, out):
    out[...] = vec[...]


def beta_first_kernel(chunk, pos, pat, vec, near, far, out, held, prod):
    half = pos[1]
    for k in range(K):
        t = (k // 2) ^ pos[0]

        @pl.when(half == k % 2)
        def _(k=k, t=t):
            held[k] = near[t]

        @pl.when(half != k % 2)
        def _(k=k, t=t):
            held[k] = far[t]

    lhs = jnp.concatenate(
        [
            held[k, s * 32 + chunk * 16 : s * 32 + chunk * 16 + 16, :]
            for k in range(K)
            for s in range(S)
        ],
        axis=0,
    )

    def products(q, carry):
        pair = vec[:, pl.ds(pl.multiple_of(q * 256, 256), 256)]
        rhs = jnp.concatenate([pair[:, :BLK], pair[:, BLK:]], axis=0)
        r = lax.dot_general(lhs, rhs, NT, preferred_element_type=f32)
        prod[2 * q] = r[:, :BLK]
        prod[2 * q + 1] = r[:, BLK:]
        return carry

    lax.fori_loop(0, NBB // 2, products, 0, unroll=16)
    where = [place(pos, k) * (S * NBB) for k in range(K)]

    def collect(d, carry):
        x, y = d // 4, d % 4
        for zh in range(2):
            j = 2 * (8 * x + 4 * zh + y) + half
            for k in range(K):
                base = where[k] + j
                t = [
                    prod[pat[base + s * NBB], k * 64 + s * 16 : k * 64 + s * 16 + 16, :]
                    for s in range(S)
                ]
                out[d, k, zh] = ((t[0] + t[1]) + (t[2] + t[3])).astype(bf16)
        return carry

    lax.fori_loop(0, 16, collect, 0, unroll=2)


def alpha_first_kernel(pos, slot, img, tiles, send, keep, prod, acc):
    zh = pos[3]
    for t in range(4):
        prod[t, 16] = jnp.zeros((32, 512), f32)
    acc[...] = jnp.zeros_like(acc)

    def factors(g, carry):
        for t in range(4):
            rhs = tiles[4 * g + t, :S].reshape(512, BLK)
            for q in range(2):
                lhs = img[8 * q : 8 * q + 8, 4 * g + t].reshape(256, BLK)
                r = lax.dot_general(lhs, rhs, NT, preferred_element_type=f32)
                prod[t, 8 * q : 8 * q + 8] = r.reshape(8, 32, 512)

        bases = [place(pos, 4 * g + t) * (S * NAB) for t in range(4)]

        def collect(i, carry):
            a = acc[i]
            for t in range(4):
                for s in range(S):
                    at = slot[bases[t] + s * NAB + i]
                    a += prod[t, at, :, s * BLK : s * BLK + BLK]
            acc[i] = a
            return carry

        lax.fori_loop(0, NAB, collect, 0, unroll=8)
        return carry

    lax.fori_loop(0, K // 4, factors, 0)
    own = pl.multiple_of(zh * 16, 16)
    other = pl.multiple_of((1 - zh) * 16, 16)
    keep[...] = acc[:, pl.ds(own, 16), :]
    send[...] = acc[:, pl.ds(other, 16), :].astype(bf16)


def first_kernel(chunk, pos, energy, asec, bsec, keep, recv, adiag, bdiag, out):
    string, ze, c = pos[4], pos[2], pos[1]
    block = 2 * string + c
    lane = lax.broadcasted_iota(jnp.int32, (16, BLK), 1)
    want = lax.broadcasted_iota(jnp.int32, (16, BLK), 0) + (ze * 32 + chunk * 16)
    row = bdiag[pl.ds(block, 1), :]
    bcol = jnp.sum(jnp.where(lane == want, row, 0.0), axis=1, keepdims=True) - energy[0]
    label = bsec[block]

    def rows(i, carry):
        den = adiag[pl.ds(i, 1), :] + bcol
        live = jnp.where(asec[i] == label, 1.0, 0.0)
        out[i] = (live * (keep[i] + recv[i].astype(f32)) / den).astype(bf16)
        return carry

    lax.fori_loop(0, NAB, rows, 0, unroll=4)


def alpha_second_kernel(
    pos, pat, u0, u1, u2, u3, v0, v1, v2, v3, tiles, out, weight, prod, cols
):
    zh, ze, zl = pos[3], pos[2], pos[0]
    row = pl.multiple_of(ze * 32, 32)
    for k in range(K):
        weight[k] = tiles[k, :S, pl.ds(row, 32), :]
    for t, (ua, ub) in enumerate(((u0, v0), (u1, v1), (u2, v2), (u3, v3))):
        for at in range(4):

            @pl.when(ze == at ^ t)
            def _(ua=ua, ub=ub, at=at):
                cols[:, at * 32 : at * 32 + 16, :] = ua[...]
                cols[:, at * 32 + 16 : at * 32 + 32, :] = ub[...]


    def products(q, carry):
        rhs = cols[pl.ds(2 * q, 2)].reshape(256, BLK)
        for g in range(2):
            lhs = weight[4 * g : 4 * g + 4].reshape(512, BLK)
            r = lax.dot_general(lhs, rhs, NT, preferred_element_type=f32)
            prod[2 * q, g * 512 : g * 512 + 512, :] = r[:, :BLK]
            prod[2 * q + 1, g * 512 : g * 512 + 512, :] = r[:, BLK:]
        return carry

    lax.fori_loop(0, NAB // 2, products, 0, unroll=16)
    where = [place(pos, k) * (S * NAB) for k in range(K)]

    def collect(d, carry):
        x, y = d // 4, d % 4
        for w in range(2):
            for k in range(K):
                base = where[k] + (8 * x + 4 * w + y)
                a = prod[pat[base], k * 128 : k * 128 + 32, :]
                for s in range(1, S):
                    a += prod[pat[base + s * NAB], k * 128 + s * 32 : k * 128 + s * 32 + 32, :]
                a = a.astype(bf16)
                out[2 * d, k, w] = a[:16]
                out[2 * d + 1, k, w] = a[16:]
        return carry

    lax.fori_loop(0, 16, collect, 0, unroll=2)

def edge_kernel(pos, u0, u1, u2, u3, v0, v1, v2, v3, mine, theirs, cols):
    zl, c, ze = pos[0], pos[1], pos[2]
    for out, core in ((mine, c), (theirs, 1 - c)):
        first = 4 * (2 * zl + core)
        for t, (ua, ub) in enumerate(((u0, v0), (u1, v1), (u2, v2), (u3, v3))):
            for at in range(4):

                @pl.when(ze == at ^ t)
                def _(ua=ua, ub=ub, at=at, first=first):
                    cols[:, at * 32 : at * 32 + 16, :] = ua[pl.ds(first, 4)]
                    cols[:, at * 32 + 16 : at * 32 + 32, :] = ub[pl.ds(first, 4)]

        for t in range(4):
            out[t * BLK : t * BLK + BLK, :] = cols[t].astype(f32).T.astype(bf16)


def beta_second_kernel(pos, slot, img, tiles, out, prod, acc):
    for t in range(4):
        prod[t, 32] = jnp.zeros((32, 512), f32)
    acc[...] = jnp.zeros_like(acc)

    def factors(g, carry):
        for t in range(4):
            rhs = jnp.concatenate([tiles[4 * g + t, S + s] for s in range(S)], axis=1)
            for q in range(4):
                lhs = img[8 * q : 8 * q + 8, 4 * g + t].reshape(256, BLK)
                r = lax.dot_general(lhs, rhs, NN, preferred_element_type=f32)
                prod[t, 8 * q : 8 * q + 8] = r.reshape(8, 32, 512)

        bases = [place(pos, 4 * g + t) * (S * NBB) for t in range(4)]

        def collect(j, carry):
            a = acc[j]
            for t in range(4):
                for s in range(S):
                    at = slot[bases[t] + s * NBB + j]
                    a += prod[t, at, :, s * BLK : s * BLK + BLK]
            acc[j] = a
            return carry

        lax.fori_loop(0, NBB, collect, 0, unroll=8)
        return carry

    lax.fori_loop(0, K // 4, factors, 0)
    for f in range(8):
        part = acc[8 * f : 8 * f + 8].astype(bf16)
        out[f, 0] = part[:, :16]
        out[f, 1] = part[:, 16:]


def second_kernel(live, recv, acol, brow, out):
    for ze in range(4):
        for c in range(2):
            g = 2 * ze + c
            a = acol[16 * g : 16 * g + 16, :]
            for j in range(8):
                one = recv[2 * g, j].astype(f32)
                two = recv[2 * (2 * (3 - ze) + c) + 1, j].astype(f32)
                den = a + brow[:, j * BLK : j * BLK + BLK]
                out[16 * g : 16 * g + 16, j * BLK : j * BLK + BLK] = (
                    live[j] * (one + two) / den
                ).astype(bf16)


def body(
    vector,
    alpha_tiles,
    alpha_pattern,
    beta_tiles,
    beta_pattern,
    alpha_sector,
    beta_sector,
    alpha_diag,
    beta_diag,
    energy,
):
    zl, c, x, zh, y = (lax.axis_index(a) for a in ALL)
    ze = zl + zh * (3 - 2 * zl)
    string = 8 * x + 4 * zh + y
    fac = 2 * zl + c
    pos = jnp.stack([zl, c, ze, zh, string]).astype(jnp.int32)

    *packed, both = call(
        pack_kernel,
        [jax.ShapeDtypeStruct((PAY, BLK), bf16)] * 4
        + [jax.ShapeDtypeStruct((2 * S, BLK, BLK), bf16)],
        [SM, HB, HB, VM, VM],
        [
            pltpu.VMEM((S, BLK, BLK), bf16),
            pltpu.VMEM((16, BLK), f32),
            pltpu.SemaphoreType.DMA((2,)),
        ],
        us=1,
        mib=58,
    )(pos, alpha_tiles[0], beta_tiles[0], alpha_pattern[0].T, beta_pattern[0].T)
    tiles = lax.all_gather(both, FAC, axis=0, tiled=False)
    near = [packed[0]] + [lax.ppermute(packed[t], ALL, BESIDE[t]) for t in (1, 2, 3)]
    near = jnp.stack(near)
    vector = call(hold_kernel, jax.ShapeDtypeStruct((BLK, NBB * BLK), bf16), [VM], us=2, mib=6)(vector)
    near, vector = lax.optimization_barrier((near, vector))
    far = lax.ppermute(near, ALL, SIBLING)
    pats = jnp.concatenate([near[:, 128:PAY], far[:, 128:PAY]], axis=0).astype(jnp.int32)
    bpat = pats[:, :S, :NBB].reshape(-1)
    apat = pats[:, 8 : 8 + S, :NAB].reshape(-1)
    aslot = jnp.where((apat >> 2) % 2 == zh, ((apat >> 3) << 2) + apat % 4, 16)
    bslot = jnp.where(
        (bpat >> 3) % 2 == zh, bpat % 2 + 2 * (((bpat >> 4) << 2) + (bpat >> 1) % 4), 32
    )

    adiag = alpha_diag.reshape(NAB, BLK)
    bdiag = beta_diag.reshape(NBB, BLK)

    gathered = []
    for chunk in range(2):
        image = call(
            functools.partial(beta_first_kernel, chunk),
            jax.ShapeDtypeStruct((16, K, 2, 16, BLK), bf16),
            [SM, SM, VM, VM, VM],
            [pltpu.VMEM((K, PAY, BLK), bf16), pltpu.VMEM((NBB, 512, BLK), f32)],
            us=5,
            mib=24,
        )(pos, bpat, vector, near, far)
        image = lax.all_to_all(image, ("x", "y"), split_axis=0, concat_axis=0, tiled=True)
        send, keep = call(
            alpha_first_kernel,
            [
                jax.ShapeDtypeStruct((NAB, 16, BLK), bf16),
                jax.ShapeDtypeStruct((NAB, 16, BLK), f32),
            ],
            [SM, SM, VM, VM],
            [pltpu.VMEM((4, 17, 32, 512), f32), pltpu.VMEM((NAB, 32, BLK), f32)],
            us=4,
            mib=14,
        )(pos, aslot, image, tiles)
        got = lax.ppermute(send, ALL, MIRROR)
        u = call(
            functools.partial(first_kernel, chunk),
            jax.ShapeDtypeStruct((NAB, 16, BLK), bf16),
            [SM, SM, SM, SM, VM, VM, VM, VM],
            us=1,
            mib=6,
        )(pos, energy, alpha_sector, beta_sector, keep, got, adiag, bdiag)
        one, two = (lax.ppermute(u, ALL, BESIDE[t]) for t in (1, 2))
        gathered += [u, one, two, lax.ppermute(two, ALL, BESIDE[1])]

    mine, theirs = call(
        edge_kernel,
        [jax.ShapeDtypeStruct((512, BLK), bf16)] * 2,
        [SM] + [VM] * 8,
        [pltpu.VMEM((4, BLK, BLK), bf16)],
        us=1,
        mib=6,
    )(pos, *gathered)
    back = call(
        alpha_second_kernel,
        jax.ShapeDtypeStruct((32, K, 2, 16, BLK), bf16),
        [SM, SM] + [VM] * 9,
        [
            pltpu.VMEM((K, S, 32, BLK), bf16),
            pltpu.VMEM((NAB, K * S * 32, BLK), f32),
            pltpu.VMEM((NAB, BLK, BLK), bf16),
        ],
        us=5,
        mib=28,
    )(pos, apat, *gathered, tiles)
    other = lax.ppermute(theirs, ALL, SIBLING)
    first_update = jnp.where(
        c == 0,
        jnp.concatenate([mine, other], axis=1),
        jnp.concatenate([other, mine], axis=1),
    )

    back = lax.all_to_all(back, ("x", "y", "c"), split_axis=0, concat_axis=0, tiled=True)
    part = call(
        beta_second_kernel,
        jax.ShapeDtypeStruct((8, 2, 8, 16, BLK), bf16),
        [SM, SM, VM, VM],
        [pltpu.VMEM((4, 33, 32, 512), f32), pltpu.VMEM((NBB, 32, BLK), f32)],
        us=7,
        mib=20,
    )(pos, bslot, back, tiles)
    part = part.reshape(16, 8, 16, BLK)
    part = lax.all_to_all(part, ("zl", "c", "zh"), split_axis=0, concat_axis=0, tiled=True)
    labels = lax.dynamic_slice_in_dim(beta_sector, fac * 8, 8)
    live_cols = (labels == lax.dynamic_index_in_dim(alpha_sector, string, keepdims=False)).astype(f32)
    acol = lax.dynamic_slice_in_dim(alpha_diag, string * BLK, BLK) - energy[0]
    brow = lax.dynamic_slice_in_dim(beta_diag, fac * 1024, 1024)
    second_update = call(
        second_kernel,
        jax.ShapeDtypeStruct((BLK, 1024), bf16),
        [SM, VM, VM, VM],
        us=1,
        mib=8,
    )(live_cols, part, acol.reshape(BLK, 1), brow.reshape(1, 1024))
    return (first_update, second_update)


def solution(mesh):
    finer = Mesh(mesh.devices.reshape(SIZES), ALL)
    strings = ("x", "zh", "y")
    in_specs = (
        P(strings, None),
        P(FAC, None, None, None),
        P(FAC, None, None),
        P(FAC, None, None, None),
        P(FAC, None, None),
        P(),
        P(),
        P(),
        P(),
        P(),
    )
    out_specs = (P(FAC, strings), P(strings, FAC))
    return jax.shard_map(body, mesh=finer, in_specs=in_specs, out_specs=out_specs, check_vma=False)
```

```python
import functools
import itertools

import jax
import jax.numpy as jnp
import numpy as np
from jax import lax
from jax.experimental import pallas as pl
from jax.experimental.pallas import tpu as pltpu
from jax.sharding import Mesh
from jax.sharding import PartitionSpec as P

ALL = ("zl", "c", "x", "zh", "y")
FAC = ("zl", "c")
SIZES = (4, 2, 4, 2, 4)
K, S, BLK, NAB, NBB = 8, 4, 128, 32, 64
PAY = 144
f32, bf16 = jnp.float32, jnp.bfloat16

NT = (((1,), (1,)), ((), ()))
NN = (((1,), (0,)), ((), ()))


def permutation(move):
    index = np.arange(256).reshape(SIZES)
    places = itertools.product(*(range(n) for n in SIZES))
    return [(int(index[p]), int(index[move(*p)])) for p in places]


MIRROR = permutation(lambda zl, c, x, zh, y: (3 - zl, c, x, 1 - zh, y))
BESIDE = [permutation(lambda zl, c, x, zh, y, t=t: (zl ^ t, c, x, zh, y)) for t in range(4)]
SIBLING = permutation(lambda zl, c, x, zh, y: (zl, 1 - c, x, zh, y))

VM = pl.BlockSpec(memory_space=pltpu.VMEM)
HB = pl.BlockSpec(memory_space=pl.ANY)
SM = pl.BlockSpec(memory_space=pltpu.SMEM)


def call(kernel, out_shape, in_specs, scratch=(), mib=40, us=2, outs=None):
    many = isinstance(out_shape, (list, tuple))
    return pl.pallas_call(
        kernel,
        out_shape=out_shape,
        in_specs=in_specs,
        out_specs=outs or ([VM] * len(out_shape) if many else VM),
        scratch_shapes=list(scratch),
        cost_estimate=pl.CostEstimate(flops=0, transcendentals=0, bytes_accessed=us * 3_000_000),
        compiler_params=pltpu.CompilerParams(vmem_limit_bytes=mib << 20),
    )


def place(pos, k):
    return 4 * ((k % 2) ^ pos[1]) + ((k // 2) ^ pos[0])


def pack_kernel(pos, alpha, beta, apat, bpat, o0, o1, o2, o3, both, turned, tail, sem):
    ze = pos[2]
    outs = (o0, o1, o2, o3)
    copies = [
        pltpu.make_async_copy(alpha, both.at[pl.ds(0, S)], sem.at[0]),
        pltpu.make_async_copy(beta, both.at[pl.ds(S, S)], sem.at[1]),
    ]
    for copy in copies:
        copy.start()
    tail[...] = jnp.zeros_like(tail)
    tail[:S, :NBB] = bpat[...].astype(f32)
    tail[8 : 8 + S, :NAB] = apat[...].astype(f32)
    last = tail[...].astype(bf16)
    for copy in copies:
        copy.wait()
    for s in range(S):
        turned[s] = both[S + s].astype(f32).T.astype(bf16)
    for t in range(4):
        quarter = ze ^ t
        for s in range(S):
            part = turned[s, pl.ds(pl.multiple_of(quarter * 32, 32), 32), :]
            outs[t][s * 32 : s * 32 + 32, :] = part
        outs[t][128:PAY, :] = last


def hold_kernel(vec, out):
    out[...] = vec[...]


def beta_first_kernel(chunk, pos, pat, vec, near, far, out, held, prod):
    half = pos[1]
    for k in range(K):
        t = (k // 2) ^ pos[0]

        @pl.when(half == k % 2)
        def _(k=k, t=t):
            held[k] = near[t]

        @pl.when(half != k % 2)
        def _(k=k, t=t):
            held[k] = far[t]

    lhs = jnp.concatenate(
        [
            held[k, s * 32 + chunk * 16 : s * 32 + chunk * 16 + 16, :]
            for k in range(K)
            for s in range(S)
        ],
        axis=0,
    )

    def products(q, carry):
        pair = vec[:, pl.ds(pl.multiple_of(q * 256, 256), 256)]
        rhs = jnp.concatenate([pair[:, :BLK], pair[:, BLK:]], axis=0)
        r = lax.dot_general(lhs, rhs, NT, preferred_element_type=f32)
        prod[2 * q] = r[:, :BLK]
        prod[2 * q + 1] = r[:, BLK:]
        return carry

    lax.fori_loop(0, NBB // 2, products, 0, unroll=32)
    where = [place(pos, k) * (S * NBB) for k in range(K)]

    def collect(d, carry):
        x, y = d // 4, d % 4
        for zh in range(2):
            j = 2 * (8 * x + 4 * zh + y) + half
            for k in range(K):
                base = where[k] + j
                t = [
                    prod[pat[base + s * NBB], k * 64 + s * 16 : k * 64 + s * 16 + 16, :]
                    for s in range(S)
                ]
                out[d, k, zh] = ((t[0] + t[1]) + (t[2] + t[3])).astype(bf16)
        return carry

    lax.fori_loop(0, 16, collect, 0, unroll=2)


def alpha_first_kernel(pos, slot, img, tiles, send, keep, prod, acc):
    zh = pos[3]
    for t in range(4):
        prod[t, 16] = jnp.zeros((32, 512), f32)
    acc[...] = jnp.zeros_like(acc)

    def factors(g, carry):
        for t in range(4):
            rhs = tiles[4 * g + t, :S].reshape(512, BLK)
            for q in range(2):
                lhs = img[8 * q : 8 * q + 8, 4 * g + t].reshape(256, BLK)
                r = lax.dot_general(lhs, rhs, NT, preferred_element_type=f32)
                prod[t, 8 * q : 8 * q + 8] = r.reshape(8, 32, 512)

        bases = [place(pos, 4 * g + t) * (S * NAB) for t in range(4)]

        def collect(i, carry):
            a = acc[i]
            for t in range(4):
                for s in range(S):
                    at = slot[bases[t] + s * NAB + i]
                    a += prod[t, at, :, s * BLK : s * BLK + BLK]
            acc[i] = a
            return carry

        lax.fori_loop(0, NAB, collect, 0, unroll=8)
        return carry

    lax.fori_loop(0, K // 4, factors, 0)
    own = pl.multiple_of(zh * 16, 16)
    other = pl.multiple_of((1 - zh) * 16, 16)
    keep[...] = acc[:, pl.ds(own, 16), :]
    send[...] = acc[:, pl.ds(other, 16), :].astype(bf16)


def first_kernel(chunk, pos, energy, asec, bsec, keep, recv, adiag, bdiag, out):
    string, ze, c = pos[4], pos[2], pos[1]
    block = 2 * string + c
    lane = lax.broadcasted_iota(jnp.int32, (16, BLK), 1)
    want = lax.broadcasted_iota(jnp.int32, (16, BLK), 0) + (ze * 32 + chunk * 16)
    row = bdiag[pl.ds(block, 1), :]
    bcol = jnp.sum(jnp.where(lane == want, row, 0.0), axis=1, keepdims=True) - energy[0]
    label = bsec[block]

    def rows(i, carry):
        den = adiag[pl.ds(i, 1), :] + bcol
        live = jnp.where(asec[i] == label, 1.0, 0.0)
        out[i] = (live * (keep[i] + recv[i].astype(f32)) / den).astype(bf16)
        return carry

    lax.fori_loop(0, NAB, rows, 0, unroll=4)


def alpha_second_kernel(
    pos, pat, u0, u1, u2, u3, v0, v1, v2, v3, tiles, out, weight, prod, cols
):
    zh, ze, zl = pos[3], pos[2], pos[0]
    row = pl.multiple_of(ze * 32, 32)
    for k in range(K):
        weight[k] = tiles[k, :S, pl.ds(row, 32), :]
    for t, (ua, ub) in enumerate(((u0, v0), (u1, v1), (u2, v2), (u3, v3))):
        for at in range(4):

            @pl.when(ze == at ^ t)
            def _(ua=ua, ub=ub, at=at):
                cols[:, at * 32 : at * 32 + 16, :] = ua[...]
                cols[:, at * 32 + 16 : at * 32 + 32, :] = ub[...]


    def products(q, carry):
        rhs = cols[pl.ds(2 * q, 2)].reshape(256, BLK)
        for g in range(2):
            lhs = weight[4 * g : 4 * g + 4].reshape(512, BLK)
            r = lax.dot_general(lhs, rhs, NT, preferred_element_type=f32)
            prod[2 * q, g * 512 : g * 512 + 512, :] = r[:, :BLK]
            prod[2 * q + 1, g * 512 : g * 512 + 512, :] = r[:, BLK:]
        return carry

    lax.fori_loop(0, NAB // 2, products, 0, unroll=16)
    where = [place(pos, k) * (S * NAB) for k in range(K)]

    def collect(d, carry):
        x, y = d // 4, d % 4
        for w in range(2):
            for k in range(K):
                base = where[k] + (8 * x + 4 * w + y)
                a = prod[pat[base], k * 128 : k * 128 + 32, :]
                for s in range(1, S):
                    a += prod[pat[base + s * NAB], k * 128 + s * 32 : k * 128 + s * 32 + 32, :]
                a = a.astype(bf16)
                out[2 * d, k, w] = a[:16]
                out[2 * d + 1, k, w] = a[16:]
        return carry

    lax.fori_loop(0, 16, collect, 0, unroll=2)

def edge_kernel(pos, u0, u1, u2, u3, v0, v1, v2, v3, mine, theirs, cols):
    zl, c, ze = pos[0], pos[1], pos[2]
    for out, core in ((mine, c), (theirs, 1 - c)):
        first = 4 * (2 * zl + core)
        for t, (ua, ub) in enumerate(((u0, v0), (u1, v1), (u2, v2), (u3, v3))):
            for at in range(4):

                @pl.when(ze == at ^ t)
                def _(ua=ua, ub=ub, at=at, first=first):
                    cols[:, at * 32 : at * 32 + 16, :] = ua[pl.ds(first, 4)]
                    cols[:, at * 32 + 16 : at * 32 + 32, :] = ub[pl.ds(first, 4)]

        for t in range(4):
            out[t * BLK : t * BLK + BLK, :] = cols[t].astype(f32).T.astype(bf16)


def beta_second_kernel(pos, slot, img, tiles, out, prod, acc):
    for t in range(4):
        prod[t, 32] = jnp.zeros((32, 512), f32)
    acc[...] = jnp.zeros_like(acc)

    def factors(g, carry):
        for t in range(4):
            rhs = jnp.concatenate([tiles[4 * g + t, S + s] for s in range(S)], axis=1)
            for q in range(4):
                lhs = img[8 * q : 8 * q + 8, 4 * g + t].reshape(256, BLK)
                r = lax.dot_general(lhs, rhs, NN, preferred_element_type=f32)
                prod[t, 8 * q : 8 * q + 8] = r.reshape(8, 32, 512)

        bases = [place(pos, 4 * g + t) * (S * NBB) for t in range(4)]

        def collect(j, carry):
            a = acc[j]
            for t in range(4):
                for s in range(S):
                    at = slot[bases[t] + s * NBB + j]
                    a += prod[t, at, :, s * BLK : s * BLK + BLK]
            acc[j] = a
            return carry

        lax.fori_loop(0, NBB, collect, 0, unroll=8)
        return carry

    lax.fori_loop(0, K // 4, factors, 0)
    for f in range(8):
        part = acc[8 * f : 8 * f + 8].astype(bf16)
        out[f, 0] = part[:, :16]
        out[f, 1] = part[:, 16:]


def second_kernel(live, recv, acol, brow, out):
    for ze in range(4):
        for c in range(2):
            g = 2 * ze + c
            a = acol[16 * g : 16 * g + 16, :]
            for j in range(8):
                one = recv[2 * g, j].astype(f32)
                two = recv[2 * (2 * (3 - ze) + c) + 1, j].astype(f32)
                den = a + brow[:, j * BLK : j * BLK + BLK]
                out[16 * g : 16 * g + 16, j * BLK : j * BLK + BLK] = (
                    live[j] * (one + two) / den
                ).astype(bf16)


def body(
    vector,
    alpha_tiles,
    alpha_pattern,
    beta_tiles,
    beta_pattern,
    alpha_sector,
    beta_sector,
    alpha_diag,
    beta_diag,
    energy,
):
    zl, c, x, zh, y = (lax.axis_index(a) for a in ALL)
    ze = zl + zh * (3 - 2 * zl)
    string = 8 * x + 4 * zh + y
    fac = 2 * zl + c
    pos = jnp.stack([zl, c, ze, zh, string]).astype(jnp.int32)

    *packed, both = call(
        pack_kernel,
        [jax.ShapeDtypeStruct((PAY, BLK), bf16)] * 4
        + [jax.ShapeDtypeStruct((2 * S, BLK, BLK), bf16)],
        [SM, HB, HB, VM, VM],
        [
            pltpu.VMEM((S, BLK, BLK), bf16),
            pltpu.VMEM((16, BLK), f32),
            pltpu.SemaphoreType.DMA((2,)),
        ],
        us=1,
        mib=58,
    )(pos, alpha_tiles[0], beta_tiles[0], alpha_pattern[0].T, beta_pattern[0].T)
    tiles = lax.all_gather(both, FAC, axis=0, tiled=False)
    near = [packed[0]] + [lax.ppermute(packed[t], ALL, BESIDE[t]) for t in (1, 2, 3)]
    near = jnp.stack(near)
    vector = call(hold_kernel, jax.ShapeDtypeStruct((BLK, NBB * BLK), bf16), [VM], us=2, mib=6)(vector)
    near, vector = lax.optimization_barrier((near, vector))
    far = lax.ppermute(near, ALL, SIBLING)
    pats = jnp.concatenate([near[:, 128:PAY], far[:, 128:PAY]], axis=0).astype(jnp.int32)
    bpat = pats[:, :S, :NBB].reshape(-1)
    apat = pats[:, 8 : 8 + S, :NAB].reshape(-1)
    aslot = jnp.where((apat >> 2) % 2 == zh, ((apat >> 3) << 2) + apat % 4, 16)
    bslot = jnp.where(
        (bpat >> 3) % 2 == zh, bpat % 2 + 2 * (((bpat >> 4) << 2) + (bpat >> 1) % 4), 32
    )

    adiag = alpha_diag.reshape(NAB, BLK)
    bdiag = beta_diag.reshape(NBB, BLK)

    gathered = []
    for chunk in range(2):
        image = call(
            functools.partial(beta_first_kernel, chunk),
            jax.ShapeDtypeStruct((16, K, 2, 16, BLK), bf16),
            [SM, SM, VM, VM, VM],
            [pltpu.VMEM((K, PAY, BLK), bf16), pltpu.VMEM((NBB, 512, BLK), f32)],
            us=5,
            mib=24,
        )(pos, bpat, vector, near, far)
        image = lax.all_to_all(image, ("x", "y"), split_axis=0, concat_axis=0, tiled=True)
        send, keep = call(
            alpha_first_kernel,
            [
                jax.ShapeDtypeStruct((NAB, 16, BLK), bf16),
                jax.ShapeDtypeStruct((NAB, 16, BLK), f32),
            ],
            [SM, SM, VM, VM],
            [pltpu.VMEM((4, 17, 32, 512), f32), pltpu.VMEM((NAB, 32, BLK), f32)],
            us=4,
            mib=14,
        )(pos, aslot, image, tiles)
        got = lax.ppermute(send, ALL, MIRROR)
        u = call(
            functools.partial(first_kernel, chunk),
            jax.ShapeDtypeStruct((NAB, 16, BLK), bf16),
            [SM, SM, SM, SM, VM, VM, VM, VM],
            us=1,
            mib=6,
        )(pos, energy, alpha_sector, beta_sector, keep, got, adiag, bdiag)
        one, two = (lax.ppermute(u, ALL, BESIDE[t]) for t in (1, 2))
        gathered += [u, one, two, lax.ppermute(two, ALL, BESIDE[1])]

    mine, theirs = call(
        edge_kernel,
        [jax.ShapeDtypeStruct((512, BLK), bf16)] * 2,
        [SM] + [VM] * 8,
        [pltpu.VMEM((4, BLK, BLK), bf16)],
        us=1,
        mib=6,
    )(pos, *gathered)
    back = call(
        alpha_second_kernel,
        jax.ShapeDtypeStruct((32, K, 2, 16, BLK), bf16),
        [SM, SM] + [VM] * 9,
        [
            pltpu.VMEM((K, S, 32, BLK), bf16),
            pltpu.VMEM((NAB, K * S * 32, BLK), f32),
            pltpu.VMEM((NAB, BLK, BLK), bf16),
        ],
        us=5,
        mib=28,
    )(pos, apat, *gathered, tiles)
    other = lax.ppermute(theirs, ALL, SIBLING)
    first_update = jnp.where(
        c == 0,
        jnp.concatenate([mine, other], axis=1),
        jnp.concatenate([other, mine], axis=1),
    )

    back = lax.all_to_all(back, ("x", "y", "c"), split_axis=0, concat_axis=0, tiled=True)
    part = call(
        beta_second_kernel,
        jax.ShapeDtypeStruct((8, 2, 8, 16, BLK), bf16),
        [SM, SM, VM, VM],
        [pltpu.VMEM((4, 33, 32, 512), f32), pltpu.VMEM((NBB, 32, BLK), f32)],
        us=7,
        mib=20,
    )(pos, bslot, back, tiles)
    part = part.reshape(16, 8, 16, BLK)
    part = lax.all_to_all(part, ("zl", "c", "zh"), split_axis=0, concat_axis=0, tiled=True)
    labels = lax.dynamic_slice_in_dim(beta_sector, fac * 8, 8)
    live_cols = (labels == lax.dynamic_index_in_dim(alpha_sector, string, keepdims=False)).astype(f32)
    acol = lax.dynamic_slice_in_dim(alpha_diag, string * BLK, BLK) - energy[0]
    brow = lax.dynamic_slice_in_dim(beta_diag, fac * 1024, 1024)
    second_update = call(
        second_kernel,
        jax.ShapeDtypeStruct((BLK, 1024), bf16),
        [SM, VM, VM, VM],
        us=1,
        mib=8,
    )(live_cols, part, acol.reshape(BLK, 1), brow.reshape(1, 1024))
    return (first_update, second_update)


def solution(mesh):
    finer = Mesh(mesh.devices.reshape(SIZES), ALL)
    strings = ("x", "zh", "y")
    in_specs = (
        P(strings, None),
        P(FAC, None, None, None),
        P(FAC, None, None),
        P(FAC, None, None, None),
        P(FAC, None, None),
        P(),
        P(),
        P(),
        P(),
        P(),
    )
    out_specs = (P(FAC, strings), P(strings, FAC))
    return jax.shard_map(body, mesh=finer, in_specs=in_specs, out_specs=out_specs, check_vma=False)
```
